128 devices in a mesh: sub: 128 (over z, x, y, core).
Axes of the slice: x: 4, y: 4, z: 4, core: 2. Of those that a mesh axis runs over, the one named last changes fastest.
Arguments:
- load: float32 [16, 256, 512], P(None, 'sub'), may hold values from -6 to 6
- schur_inverse: float32 [256, 512, 512], P('sub'), may hold values from -1 to 2, as said below
- schur: float32 [256, 512, 512], P('sub'), may hold values from -1 to 8, as said below
- corner_map: float32 [256, 24, 512], P('sub'), may hold values from -0.25 to 0.25
- corner_ids: int32 [256, 24], P('sub'), may hold values from 0 to 3071
- coarse_inverse: float32 [3072, 72], P('sub'), may hold values from -1 to 2, as said below
- partner: int32 [256, 512], P('sub'), may hold values from 0 to 131071, as said below
Outputs:
- multipliers: float32 [16, 256, 512], P(None, 'sub')
- residual: float32 [16, 256, 512], P(None, 'sub')
The draws below stay inside these ranges and needn't reach their ends.
Inputs may be any that keep to these rules, and one draw needn't show every extreme that they name: `schur_inverse`: symmetric positive definite blocks. `schur`: symmetric positive definite blocks. `coarse_inverse`: the matrix that these rows form is symmetric, block tridiagonal over owners and diagonally dominant; the columns of the owner before the first and after the last are zero. `partner`: the pairing is mutual, no dof is paired with itself, and a dof of subdomain s is paired with a dof of a subdomain whose index differs from s by at most 1.
All inputs are finite; a program needn't handle non-finite values.
Results may differ from the reference program's by a relative error of at most 0.0003.
Values sent between devices are 32-bit elements; how exact they have to be, the bound alone decides.
A program may use at most 64 MiB of HBM per device.

```python
import jax
import jax.numpy as jnp
from jax import lax

DOFS = 512
CASES = 16
SUB_DEV = 2
CORNERS = 24
ITERS = 2
OWN_COARSE = 24
SUBS = 256
COARSE = 3072


def definite_blocks(key, count, size, lower, upper, spread):
    keys = jax.random.split(key, count)

    def single(block_key):
        first_key, second_key = jax.random.split(block_key)
        unit = jax.random.uniform(first_key, (size,), jnp.float32)
        linear = lower + (upper - lower) * unit
        diagonal = linear
        noise = jax.random.uniform(second_key, (size, size), jnp.float32, -1.0, 1.0)
        noise = 0.5 * (noise + noise.T)
        bound = spread * jnp.minimum(diagonal[:, None], diagonal[None, :]) / size
        identity = jnp.eye(size, dtype=jnp.float32)
        return noise * bound * (1.0 - identity) + diagonal[:, None] * identity
    return lax.map(single, keys)


def draw_schur_inverse(key, part):
    key = jax.random.fold_in(key, 1)
    return definite_blocks(key, SUBS, DOFS, 0.25, 2.0, 0.8)


def draw_schur(key, part):
    key = jax.random.fold_in(key, 2)
    return definite_blocks(key, SUBS, DOFS, 1.0, 8.0, 0.8)


def draw_coarse_inverse(key, part):
    key = jax.random.fold_in(key, 3)
    owners = COARSE // OWN_COARSE
    block_key, link_key = jax.random.split(key)
    middle = definite_blocks(block_key, owners, OWN_COARSE, 0.5, 2.0, 0.4)
    links = jax.random.uniform(link_key, (owners, OWN_COARSE, OWN_COARSE), jnp.float32, -1.0, 1.0)
    keep = (jnp.arange(owners) < owners - 1).astype(jnp.float32)
    upper = links * (0.125 / OWN_COARSE) * keep[:, None, None]
    lower = jnp.concatenate([jnp.zeros((1, OWN_COARSE, OWN_COARSE), jnp.float32), jnp.transpose(upper[:-1], (0, 2, 1))], axis=0)
    rows = jnp.concatenate([lower, middle, upper], axis=2)
    return rows.reshape(COARSE, 3 * OWN_COARSE)


def draw_corner_ids(key, part):
    key = jax.random.fold_in(key, 5)
    owners = COARSE // OWN_COARSE
    owner_key, slot_key = jax.random.split(key)
    owner = jax.random.randint(owner_key, (SUBS, CORNERS), 0, owners, dtype=jnp.int32)
    device = jnp.arange(owners, dtype=jnp.int32)
    firsts = device * SUB_DEV
    owner = owner.at[firsts, 0].set((device + owners // 2) % owners)
    owner = owner.at[firsts, 1].set((device + 1) % owners)
    slot = jax.random.randint(slot_key, (SUBS, CORNERS), 0, OWN_COARSE, dtype=jnp.int32)
    ids = owner * OWN_COARSE + slot
    ids = ids.at[0, 2].set(0)
    ids = ids.at[SUBS - 1, CORNERS - 1].set(COARSE - 1)
    return ids.astype(jnp.int32)


def draw_partner(key, part):
    key = jax.random.fold_in(key, 4)
    count = SUBS * DOFS
    half = DOFS // 2
    keys = jax.random.split(key, SUBS)
    orders = jax.vmap(lambda one_key: jax.random.permutation(one_key, DOFS))(keys).astype(jnp.int32)
    base = (jnp.arange(SUBS, dtype=jnp.int32) * DOFS)[:, None]
    lower = base + orders[:, :half]
    upper = base + orders[:, half:]
    result = jnp.zeros((count,), jnp.int32)
    result = result.at[upper[:-1].reshape(-1)].set(lower[1:].reshape(-1))
    result = result.at[lower[1:].reshape(-1)].set(upper[:-1].reshape(-1))
    flipped = jnp.bitwise_xor(jnp.arange(half, dtype=jnp.int32), 1)
    result = result.at[lower[0]].set(lower[0][flipped])
    result = result.at[upper[SUBS - 1]].set(upper[SUBS - 1][flipped])
    return result.reshape(SUBS, DOFS).astype(jnp.int32)


def level_of(stream_key, dims, shards, least, largest):
    level = 1.0
    for dim, blocks in shards:
        draws = jax.random.uniform(jax.random.fold_in(jax.random.fold_in(stream_key, 6), dim), (blocks,), jnp.float32, least / len(shards), largest / len(shards))
        level = level * jnp.repeat(jnp.exp(draws), dims[dim] // blocks).reshape((-1,) + (1,) * (len(dims) - 1 - dim))
    return level


def gaussian(own_key, dims, scale, limit, pieces=(), kind=jnp.bfloat16):
    entries = jax.random.normal(own_key, dims, jnp.float32) * scale
    if len(pieces) > 0:
        entries = level_of(own_key, dims, pieces, -0.22, 0.18) * entries
    return jnp.clip(entries, min=-limit, max=limit).astype(kind)


def setup_inputs(seed: int = 0) -> dict:
    seeds = jax.random.split(jax.random.key(seed), 8)
    load = gaussian(seeds[0], (CASES, SUBS, DOFS), 1.0, 6.0, ((1, 128),), jnp.float32)
    schur_inverse = draw_schur_inverse(jax.random.fold_in(seeds[7], 71), 0)
    schur = draw_schur(jax.random.fold_in(seeds[7], 71), 0)
    corner_map = gaussian(seeds[3], (SUBS, CORNERS, DOFS), DOFS ** -0.5, 0.25, ((0, 128),), jnp.float32)
    corner_ids = draw_corner_ids(jax.random.fold_in(seeds[7], 71), 0)
    coarse_inverse = draw_coarse_inverse(jax.random.fold_in(seeds[7], 71), 0)
    partner = draw_partner(jax.random.fold_in(seeds[7], 71), 0)
    return dict(load=load, schur_inverse=schur_inverse, schur=schur, corner_map=corner_map, corner_ids=corner_ids, coarse_inverse=coarse_inverse, partner=partner)


exact_precision = lax.Precision.HIGHEST


def paired(field, partner):
    flattened = field.reshape(field.shape[0], -1)
    return flattened[:, partner.reshape(-1)].reshape(field.shape)


def jumped(field, partner):
    return field - paired(field, partner)


def blockwise(matrices, field):
    return jnp.einsum("lsm,smn->lsn", field, matrices, precision=exact_precision)


def coarse_apply(assembled, coarse_inverse):
    owners = COARSE // OWN_COARSE
    grouped = assembled.reshape(CASES, owners, OWN_COARSE)
    padded = jnp.pad(grouped, ((0, 0), (1, 1), (0, 0)))
    windows = jnp.concatenate([padded[:, :-2], padded[:, 1:-1], padded[:, 2:]], axis=2)
    solved = jnp.einsum("lbj,bij->lbi", windows,
                        coarse_inverse.reshape(owners, OWN_COARSE, 3 * OWN_COARSE),
                        precision=exact_precision)
    return solved.reshape(CASES, COARSE)


def constrained(field, schur_inverse, corner_map, corner_ids, coarse_inverse):
    corner_rows = jnp.einsum("lsm,skm->lsk", field, corner_map, precision=exact_precision)
    corner_flat = corner_ids.reshape(-1)
    assembled = jnp.zeros((CASES, COARSE), jnp.float32).at[:, corner_flat].add(corner_rows.reshape(CASES, -1))
    solved = coarse_apply(assembled, coarse_inverse)
    spread_back = solved[:, corner_flat].reshape(CASES, SUBS, CORNERS)
    return blockwise(schur_inverse, field) + jnp.einsum("lsk,skm->lsm", spread_back, corner_map, precision=exact_precision)


def reference(load, schur_inverse, schur, corner_map, corner_ids, coarse_inverse, partner):
    def flexible(field):
        return jumped(constrained(jumped(field, partner), schur_inverse, corner_map, corner_ids, coarse_inverse), partner)

    def precondition(field):
        return 0.25 * jumped(blockwise(schur, jumped(field, partner)), partner)

    def products(first, second):
        return jnp.sum(first * second, axis=(1, 2))

    residual = jumped(constrained(load, schur_inverse, corner_map, corner_ids, coarse_inverse), partner)
    multipliers = jnp.zeros_like(residual)
    smoothed = precondition(residual)
    direction = smoothed
    current = products(residual, smoothed)
    for iteration in range(ITERS):
        image = flexible(direction)
        step_length = current / products(direction, image)
        multipliers = multipliers + step_length[:, None, None] * direction
        residual = residual - step_length[:, None, None] * image
        if iteration + 1 < ITERS:
            smoothed = precondition(residual)
            following = products(residual, smoothed)
            direction = smoothed + (following / current)[:, None, None] * direction
            current = following
    return multipliers, residual
```

```python
import functools
import itertools

import jax
import jax.numpy as jnp
from jax import lax
from jax.experimental import pallas as pl
from jax.experimental.pallas import tpu as pltpu
from jax.sharding import PartitionSpec as P

MESH = pl.DeviceIdType.MESH
F32, BF16, I32 = jnp.float32, jnp.bfloat16, jnp.int32
CASES, DOFS, CORNERS, OWN, WIN = 16, 512, 24, 24, 72
LANES = 128
HOPS = (0, 1, 2, 1)

OFFSETS = sorted(
    itertools.product(range(4), range(4), range(4), range(2)),
    key=lambda o: (-(HOPS[o[0]] + HOPS[o[1]] + HOPS[o[2]]), -o[3]),
)
OFFSETS.remove((0, 0, 0, 0))


def split(v):
    high = v.astype(BF16)
    return high, (v - high.astype(F32)).astype(BF16)


def await_bytes(ref, sem):
    pltpu.make_async_copy(ref, ref, sem).wait()


def dot(a, b):
    return jnp.dot(a, b, preferred_element_type=F32)


def take_lanes(values, lanes):
    return jnp.take_along_axis(values, lanes, axis=1, mode="promise_in_bounds")


def iota(shape, dim):
    return lax.broadcasted_iota(I32, shape, dim)


def kernel(
    load_hbm, inverse_hbm, schur_hbm, map_hbm, ids_hbm, coarse_hbm, partner_hbm,
    mult_ref, resid_ref,
    load_v, inverse_v, schur_v, map_v, ids_v, coarse_v, partner_v,
    inv_high, inv_low, sch_high, sch_low, map_high, map_low, map_side,
    table, id_rows, g_high, g_low, field, halo, buf1, buf2, buf3, buf4,
    in_sem, all_send, all_recv, fwd_sem, halo_send, halo_recv,
):
    me = lax.axis_index("sub")
    core, chip = me % 2, me // 2
    y, x, z = chip % 4, chip // 4 % 4, chip // 16
    zs = [(z + i) % 4 * 32 for i in range(4)]
    xs = [(x + i) % 4 * 8 for i in range(4)]
    ys = [(y + i) % 4 * 2 for i in range(4)]
    cs = [core, 1 - core]
    slot = core * 64 + chip
    right, left = (me + 1) % 128, (me + 127) % 128

    def device(o):
        return (zs[o[0]] + xs[o[1]] + ys[o[2]] + cs[o[3]],)

    def slot_of(dev):
        return dev % 2 * 64 + dev // 2

    pairs = (
        (map_hbm, map_v), (load_hbm, load_v), (ids_hbm, ids_v), (coarse_hbm, coarse_v),
        (partner_hbm, partner_v), (inverse_hbm, inverse_v), (schur_hbm, schur_v),
    )
    copies = [pltpu.make_async_copy(a, b, in_sem.at[i]) for i, (a, b) in enumerate(pairs)]
    for copy in copies:
        copy.start()

    barrier = pltpu.get_barrier_semaphore()
    for o in OFFSETS:
        pl.semaphore_signal(barrier, inc=1, device_id=device(o), device_id_type=MESH)

    lane8 = iota((8, LANES), 1)
    row8 = iota((8, LANES), 0)
    lane16 = iota((CASES, LANES), 1)
    row16 = iota((CASES, LANES), 0)

    for copy in copies[:5]:
        copy.wait()
    gap = jnp.zeros((8, DOFS), F32)
    own_maps = [map_v[s] for s in range(2)]
    for s in range(2):
        high, low = split(jnp.concatenate([own_maps[s], gap], axis=0))
        map_high[32 * (s + 1) : 32 * (s + 2)] = high
        map_low[32 * (s + 1) : 32 * (s + 2)] = low

    coarse = jnp.concatenate([coarse_v[...], jnp.zeros((OWN, LANES - WIN), F32)], axis=1)
    m0, m1, m2 = coarse[0:8], coarse[8:16], coarse[16:24]
    ids = jnp.concatenate([ids_v[...].astype(F32), jnp.zeros((2, LANES - CORNERS), F32)], axis=1)
    id_tile = jnp.full((8, LANES), -1000.0, F32)
    for s in range(2):
        row = jnp.broadcast_to(ids[s : s + 1], (8, LANES))
        for k in range(3):
            id_tile = jnp.where(row8 == 3 * s + k, pltpu.roll(row, 88 - 8 * k, 1), id_tile)
    buf1[slot, 0:8] = jnp.where(lane8 < 64, m0, pltpu.roll(m1, 64, 1))
    second = jnp.where(lane8 < 64, m2, m0)
    second = jnp.where(lane8 >= 72, pltpu.roll(m1, 8, 1), second)
    second = jnp.where(lane8 >= 80, pltpu.roll(m2, 16, 1), second)
    second = jnp.where(lane8 >= 88, id_tile, second)
    buf1[slot, 8:16] = jnp.where(lane8 >= 96, 0.0, second)

    flat = partner_v[...] - (2 * me - 1) * DOFS
    mate_block = flat // LANES
    mate_lane = flat % LANES

    def jumped(extended):
        out = []
        for s in range(2):
            columns = []
            for t in range(4):
                at = slice(t * LANES, (t + 1) * LANES)
                lanes = jnp.broadcast_to(mate_lane[s : s + 1, at], (CASES, LANES))
                block = jnp.broadcast_to(mate_block[s : s + 1, at], (CASES, LANES))
                mate = jnp.zeros((CASES, LANES), F32)
                for b in range(4 * s, 4 * s + 12):
                    source = extended[b // 4][:, b % 4 * LANES : (b % 4 + 1) * LANES]
                    mate = jnp.where(block == b, take_lanes(source, lanes), mate)
                columns.append(extended[s + 1][:, at] - mate)
            out.append(jnp.concatenate(columns, axis=1))
        return out

    def corner_rows(pair):
        tiles = []
        for s in range(2):
            high, low = split(pair[s])
            both = jnp.concatenate([high] * 8 + [low] * 8, axis=0)
            at = slice(32 * (s + 1), 32 * (s + 2))
            maps = jnp.concatenate([map_high[at], map_low[at]], axis=0)
            product = lax.dot_general(
                maps, both, (((1,), (1,)), ((), ())), preferred_element_type=F32
            )
            rows = product[0:32] + product[32:64]
            rows = rows[:, 0:LANES] + rows[:, LANES : 2 * LANES]
            for k in range(3):
                kept = jnp.where(lane8 // 16 == row8, rows[8 * k : 8 * k + 8], 0.0)
                tiles.append(jnp.sum(kept, axis=0, keepdims=True))
        out = jnp.zeros((8, LANES), F32)
        for r in range(6):
            out = jnp.where(row8 == r, tiles[r], out)
        return out

    def products(pair, other):
        total = jnp.zeros((CASES, LANES), F32)
        for s in range(2):
            product = pair[s] * other[s]
            for t in range(4):
                total = total + product[:, t * LANES : (t + 1) * LANES]
        return jnp.sum(total, axis=1, keepdims=True)

    def as_row(column, place):
        kept = jnp.where(lane16 == row16 + 16 * place, column, 0.0)
        return jnp.sum(kept, axis=0, keepdims=True)

    def as_column(row, place):
        spread = jnp.broadcast_to(row, (CASES, LANES))
        kept = jnp.where(lane16 == row16 + 16 * place, spread, 0.0)
        return jnp.sum(kept, axis=1, keepdims=True)

    def times(high, low, v, s):
        top, rest = split(v)
        both = jnp.concatenate([top, rest], axis=0)
        at = slice(DOFS * s, DOFS * s + DOFS)
        product = dot(both, high[at]) + dot(both, low[at])
        return product[0:CASES] + product[CASES : 2 * CASES]

    def cut(source, high, low):
        @pl.loop(0, 16)
        def _(i):
            at = pl.ds(pl.multiple_of(i * 64, 64), 64)
            top, rest = split(source[at])
            high[at] = top
            low[at] = rest

    def halo_copies(n):
        make = functools.partial(pltpu.make_async_remote_copy, device_id_type=MESH)
        return (
            make(src_ref=field.at[n, 1], dst_ref=halo.at[n, 0], send_sem=halo_send.at[n, 0],
                 recv_sem=halo_recv.at[n, 0], device_id=(right,)),
            make(src_ref=field.at[n, 0], dst_ref=halo.at[n, 1], send_sem=halo_send.at[n, 1],
                 recv_sem=halo_recv.at[n, 1], device_id=(left,)),
        )

    def send_halo(n, pair):
        field[n, 0] = pair[0]
        field[n, 1] = pair[1]
        for copy in halo_copies(n):
            copy.start()

    def extended(n):
        for copy in halo_copies(n):
            copy.wait()
        return [halo[n, 0], field[n, 0], field[n, 1], halo[n, 1]]

    def to_all(buf, rows, n, offsets):
        for o in offsets:
            pltpu.make_async_remote_copy(
                src_ref=buf.at[slot, pl.ds(0, rows)], dst_ref=buf.at[slot, pl.ds(0, rows)],
                send_sem=all_send.at[n], recv_sem=all_recv.at[n],
                device_id=device(o), device_id_type=MESH,
            ).start()

    load = [load_v[:, s, :] for s in range(2)]
    buf1[slot, 16:24] = corner_rows(load)

    copies[5].wait()
    cut(inverse_v, inv_high, inv_low)
    solved_load = [times(inv_high, inv_low, load[s], s) for s in range(2)]

    pl.semaphore_wait(barrier, 127)
    same_core = [o for o in OFFSETS if o[3] == 0]
    to_all(buf1, 22, 0, same_core)
    map_copies = (
        pltpu.make_async_remote_copy(
            src_ref=map_v.at[1], dst_ref=map_side.at[0], send_sem=halo_send.at[5, 0],
            recv_sem=halo_recv.at[5, 0], device_id=(right,), device_id_type=MESH),
        pltpu.make_async_remote_copy(
            src_ref=map_v.at[0], dst_ref=map_side.at[1], send_sem=halo_send.at[5, 1],
            recv_sem=halo_recv.at[5, 1], device_id=(left,), device_id_type=MESH),
    )
    for copy in map_copies:
        copy.start()
    send_halo(0, solved_load)
    copies[6].wait()
    cut(schur_v, sch_high, sch_low)
    for s, copy in enumerate(map_copies):
        copy.wait()
        high, low = split(jnp.concatenate([map_side[s], gap], axis=0))
        map_high[96 * s : 96 * s + 32] = high
        map_low[96 * s : 96 * s + 32] = low

    await_bytes(buf1.at[pl.ds(0, 63), pl.ds(0, 22)], all_recv.at[0])
    forward = pltpu.make_async_remote_copy(
        src_ref=buf1.at[pl.ds(core * 64, 64), pl.ds(0, 22)],
        dst_ref=buf1.at[pl.ds(core * 64, 64), pl.ds(0, 22)],
        send_sem=fwd_sem.at[0], recv_sem=fwd_sem.at[1],
        device_id=(zs[0] + xs[0] + ys[0] + cs[1],), device_id_type=MESH,
    )
    forward.start()
    await_bytes(buf1.at[pl.ds(0, 63), pl.ds(0, 22)], all_send.at[0])
    forward.wait()

    packed = buf1[:, 0:16, :].reshape(2048, LANES)
    id_lanes = jnp.transpose(buf1[:, 8:16, :].reshape(1024, LANES))[88:96]
    id_rows[...] = id_lanes.astype(I32)
    lane1024 = iota((8, 1024), 1)
    columns = []
    for dev, rows in ((left, (3, 4, 5)), (me, (0, 1, 2, 3, 4, 5)), (right, (0, 1, 2))):
        for r in rows:
            kept = jnp.where(lane1024 == slot_of(dev) * 8 + r, id_lanes, 0.0)
            columns.append(jnp.sum(kept, axis=1, keepdims=True))
    corner = jnp.concatenate(columns, axis=0).astype(I32)
    owner = corner // OWN
    inner = corner - owner * OWN
    third = inner // 8
    first_row = (owner % 2 * 64 + owner // 2) * 16
    row_a = first_row + inner % 8 + jnp.where(third == 2, 8, 0)
    row_t = first_row + 8 + inner % 8
    wanted = jnp.concatenate([row_a, row_t], axis=0)
    pick = jnp.where(iota((192, 2048), 1) == wanted, 1.0, 0.0).astype(BF16)
    high, low = split(packed)
    found = dot(pick, jnp.concatenate([high, low], axis=1))
    found = found[:, 0:LANES] + found[:, LANES : 2 * LANES]
    lane96 = iota((96, LANES), 1)
    from_a = take_lanes(found[0:96], jnp.minimum(lane96 + jnp.where(third == 1, 64, 0), LANES - 1))
    from_t = take_lanes(found[96:192], jnp.minimum(lane96 + 8 * third, LANES - 1))
    table[:, 0:LANES] = jnp.where(lane96 < 64, from_a, from_t)
    table[:, LANES : 2 * LANES] = jnp.broadcast_to((owner - 1) * OWN, (96, LANES)).astype(F32)

    @pl.loop(0, 48)
    def _(i):
        e, k = i // 6, i % 6
        at = pl.ds(pl.multiple_of(k * 16, 16), 16)
        rows = table[at, 0:LANES]
        base = table[at, LANES : 2 * LANES].astype(I32)
        everyone = id_rows[pl.ds(e, 1), :]
        out = pl.ds(pl.multiple_of(e * 96 + k * 16, 16), 16)
        for b in range(8):
            here = slice(b * LANES, (b + 1) * LANES)
            place = jnp.broadcast_to(everyone[:, here], (16, LANES)) - base
            inside = (place >= 0) & (place < WIN)
            entry = take_lanes(rows, jnp.where(inside, place, 0))
            top, rest = split(jnp.where(inside, entry, 0.0))
            g_high[out, here] = top
            g_low[out, here] = rest

    def spread(buf, first):
        rows = buf[:, first : first + 8, :]
        rows = jnp.where(iota((128, 8, LANES), 1) < 6, rows, 0.0).reshape(1024, LANES)
        top, rest = split(rows)
        both = jnp.concatenate([top, rest], axis=1)
        solved = jnp.zeros((96, 2 * LANES), F32)
        lanes = iota((96, 2 * LANES), 1) % LANES // 16
        for e in range(8):
            at = slice(96 * e, 96 * e + 96)
            part = dot(g_high[at], both) + dot(g_low[at], both)
            solved = jnp.where(lanes == e, part, solved)
        solved = solved[:, 0:LANES] + solved[:, LANES : 2 * LANES]
        for shift in (64, 32, 16):
            solved = solved + pltpu.roll(solved, shift, 1)
        zero = jnp.zeros((8, LANES), F32)
        padded = []
        for j in range(4):
            padded += [solved[24 * j : 24 * j + 24], zero]
        by_case = jnp.transpose(jnp.concatenate(padded, axis=0))[0:CASES]
        stack = []
        for j in range(4):
            stack += list(split(jnp.where(lane16 // 32 == j, by_case, 0.0)))
        stack = jnp.concatenate(stack, axis=0)
        product = dot(stack, map_high[...]) + dot(stack, map_low[...])
        return [product[32 * j : 32 * j + 16] + product[32 * j + 16 : 32 * j + 32] for j in range(4)]

    def add(first, second):
        return [a + b for a, b in zip(first, second)]

    def precondition(n, pair):
        send_halo(n, [times(sch_high, sch_low, pair[s], s) for s in range(2)])
        return [0.5 * v for v in jumped(extended(n))]

    r0 = jumped(add(spread(buf1, 16), extended(0)))
    a = precondition(1, r0)

    buf2[slot] = jnp.where(row8 == 6, as_row(products(r0, a), 0), corner_rows(a))
    to_all(buf2, 7, 1, OFFSETS)
    send_halo(2, [times(inv_high, inv_low, a[s], s) for s in range(2)])
    solved_a = extended(2)
    await_bytes(buf2.at[pl.ds(0, 127), pl.ds(0, 7)], all_recv.at[1])

    q = [2.0 * v for v in jumped(add(spread(buf2, 0), solved_a))]
    current = as_column(jnp.sum(buf2[:, 6, :], axis=0, keepdims=True), 0)
    w = precondition(3, q)

    buf3[slot] = jnp.where(row8 == 6, as_row(products(a, q), 0), corner_rows(w))
    to_all(buf3, 7, 2, OFFSETS)
    send_halo(4, [times(inv_high, inv_low, w[s], s) for s in range(2)])
    solved_w = extended(4)
    await_bytes(buf3.at[pl.ds(0, 127), pl.ds(0, 7)], all_recv.at[2])

    u = [2.0 * v for v in jumped(add(spread(buf3, 0), solved_w))]
    curvature = as_column(jnp.sum(buf3[:, 6, :], axis=0, keepdims=True), 0)
    step0 = current / curvature
    r1 = [r0[s] - step0 * q[s] for s in range(2)]
    z1 = [a[s] - step0 * w[s] for s in range(2)]
    image = [q[s] - step0 * u[s] for s in range(2)]
    cross = products(z1, q) + products(a, image)
    dots = as_row(products(r1, z1), 0) + as_row(products(z1, image), 1) + as_row(cross, 2)
    buf4[slot] = jnp.where(row8 == 0, dots, 0.0)
    to_all(buf4, 1, 3, OFFSETS)
    await_bytes(buf4.at[pl.ds(0, 127), pl.ds(0, 1)], all_recv.at[3])
    total = jnp.sum(buf4[:, 0, :], axis=0, keepdims=True)
    following = as_column(total, 0)
    ratio = following / current
    curvature1 = as_column(total, 1) + ratio * as_column(total, 2) + ratio * ratio * curvature
    step1 = following / curvature1
    for s in range(2):
        mult_ref[:, s, :] = step0 * a[s] + step1 * (z1[s] + ratio * a[s])
        resid_ref[:, s, :] = r1[s] - step1 * (image[s] + ratio * q[s])

    await_bytes(buf2.at[pl.ds(0, 127), pl.ds(0, 7)], all_send.at[1])
    await_bytes(buf3.at[pl.ds(0, 127), pl.ds(0, 7)], all_send.at[2])
    await_bytes(buf4.at[pl.ds(0, 127), pl.ds(0, 1)], all_send.at[3])


def per_device(load, schur_inverse, schur, corner_map, corner_ids, coarse_inverse, partner):
    vmem = pltpu.VMEM
    dma = pltpu.SemaphoreType.DMA
    matrices = (1024, DOFS)
    out = jax.ShapeDtypeStruct(load.shape, F32)

    return pl.pallas_call(
        kernel,
        out_shape=(out, out),
        in_specs=[pl.BlockSpec(memory_space=pl.ANY)] * 7,
        out_specs=(pl.BlockSpec(memory_space=vmem),) * 2,
        scratch_shapes=[
            vmem(load.shape, F32), vmem(matrices, F32), vmem(matrices, F32),
            vmem(corner_map.shape, F32), vmem(corner_ids.shape, I32),
            vmem(coarse_inverse.shape, F32), vmem(partner.shape, I32),
            vmem(matrices, BF16), vmem(matrices, BF16), vmem(matrices, BF16), vmem(matrices, BF16),
            vmem((128, DOFS), BF16), vmem((128, DOFS), BF16), vmem((2, CORNERS, DOFS), F32),
            vmem((96, 2 * LANES), F32), vmem((8, 1024), I32),
            vmem((768, 1024), BF16), vmem((768, 1024), BF16),
            vmem((5, 2, CASES, DOFS), F32), vmem((5, 2, CASES, DOFS), F32),
            vmem((128, 24, LANES), F32), vmem((128, 8, LANES), F32),
            vmem((128, 8, LANES), F32), vmem((128, 8, LANES), F32),
            dma((7,)), dma((4,)), dma((4,)), dma((2,)), dma((6, 2)), dma((6, 2)),
        ],
        compiler_params=pltpu.CompilerParams(
            collective_id=0, has_side_effects=True, vmem_limit_bytes=48 << 20
        ),
    )(
        load, schur_inverse.reshape(matrices), schur.reshape(matrices), corner_map, corner_ids,
        coarse_inverse, partner,
    )


def solution(mesh):
    in_specs = (
        P(None, "sub", None),
        P("sub", None, None),
        P("sub", None, None),
        P("sub", None, None),
        P("sub", None),
        P("sub", None),
        P("sub", None),
    )
    out_specs = (P(None, "sub", None), P(None, "sub", None))
    return jax.shard_map(
        per_device, mesh=mesh, in_specs=in_specs, out_specs=out_specs, check_vma=False
    )
```

```python
import functools
import itertools

import jax
import jax.numpy as jnp
from jax import lax
from jax.experimental import pallas as pl
from jax.experimental.pallas import tpu as pltpu
from jax.sharding import PartitionSpec as P

MESH = pl.DeviceIdType.MESH
F32, BF16, I32 = jnp.float32, jnp.bfloat16, jnp.int32
CASES, DOFS, CORNERS, OWN, WIN = 16, 512, 24, 24, 72
LANES = 128
HOPS = (0, 1, 2, 1)

CHIPS = sorted(
    itertools.product(range(4), repeat=3), key=lambda o: HOPS[o[0]] + HOPS[o[1]] + HOPS[o[2]]
)
NEAR = 57


def hops(i):
    return sum(HOPS[d] for d in CHIPS[i])


FAR_SENDS = [(64 * c + i, CHIPS[i], c) for i in range(NEAR, 64) for c in range(2)]
NEAR_SENDS = [(i, CHIPS[i], 0) for i in range(1, NEAR)]
SENDS = sorted(
    FAR_SENDS + NEAR_SENDS, key=lambda t: -(hops(t[0] % 64) + (2 if t[0] < NEAR else 0))
)
EVERYONE = sorted(
    [(64 * c + i, CHIPS[i], c) for i in range(64) for c in range(2) if i + c > 0],
    key=lambda t: -hops(t[0] % 64),
)


def split(v):
    high = v.astype(BF16)
    return high, (v - high.astype(F32)).astype(BF16)


def await_bytes(ref, sem):
    pltpu.make_async_copy(ref, ref, sem).wait()


def dot(a, b):
    return jnp.dot(a, b, preferred_element_type=F32)


def take_lanes(values, lanes):
    return jnp.take_along_axis(values, lanes, axis=1, mode="promise_in_bounds")


def iota(shape, dim):
    return lax.broadcasted_iota(I32, shape, dim)


def kernel(
    load_hbm, inverse_hbm, schur_hbm, map_hbm, ids_hbm, coarse_hbm, partner_hbm,
    mult_ref, resid_ref,
    load_v, inverse_v, schur_v, map_v, ids_v, coarse_v, partner_v,
    inverse_parts, schur_parts, map_high, map_low, map_side, id_side,
    table, bases, id_rows, operator, field, halo, coarse_buf, buf1, buf2, buf3, buf4,
    in_sem, all_send, near_recv, far_recv, fwd_send, fwd_recv, halo_send, halo_recv,
):
    me = lax.axis_index("sub")
    core, chip = me % 2, me // 2
    y, x, z = chip % 4, chip // 4 % 4, chip // 16
    zs = [(z + i) % 4 * 32 for i in range(4)]
    xs = [(x + i) % 4 * 8 for i in range(4)]
    ys = [(y + i) % 4 * 2 for i in range(4)]
    cs = [core, 1 - core]
    right, left = (me + 1) % 128, (me + 127) % 128

    def device(o, c):
        return (zs[o[0]] + xs[o[1]] + ys[o[2]] + cs[c],)

    pairs = (
        (map_hbm, map_v), (load_hbm, load_v), (ids_hbm, ids_v), (coarse_hbm, coarse_v),
        (partner_hbm, partner_v), (inverse_hbm, inverse_v), (schur_hbm, schur_v),
    )
    copies = [pltpu.make_async_copy(a, b, in_sem.at[i]) for i, (a, b) in enumerate(pairs)]
    for copy in copies:
        copy.start()

    barrier = pltpu.get_barrier_semaphore()
    for _, o, c in EVERYONE:
        pl.semaphore_signal(barrier, inc=1, device_id=device(o, c), device_id_type=MESH)

    lane8 = iota((8, LANES), 1)
    row8 = iota((8, LANES), 0)
    lane16 = iota((CASES, LANES), 1)
    row16 = iota((CASES, LANES), 0)

    for copy in copies[:5]:
        copy.wait()
    gap = jnp.zeros((8, DOFS), F32)
    own_maps = [map_v[s] for s in range(2)]
    for s in range(2):
        high, low = split(jnp.concatenate([own_maps[s], gap], axis=0))
        map_high[32 * (s + 1) : 32 * (s + 2)] = high
        map_low[32 * (s + 1) : 32 * (s + 2)] = low

    coarse = jnp.concatenate([coarse_v[...], jnp.zeros((OWN, LANES - WIN), F32)], axis=1)
    m0, m1, m2 = coarse[0:8], coarse[8:16], coarse[16:24]
    ids = jnp.concatenate([ids_v[...].astype(F32), jnp.zeros((2, LANES - CORNERS), F32)], axis=1)
    ids = jnp.where(lane8[0:1] < CORNERS, ids[0:1], pltpu.roll(ids, CORNERS, 1)[1:2])
    ids = jnp.where(lane8[0:1] < 2 * CORNERS, ids, me.astype(F32))
    coarse_buf[0, 0:8] = jnp.where(lane8 < 64, m0, pltpu.roll(m1, 64, 1))
    second = jnp.where(lane8 < 64, m2, m0)
    second = jnp.where(lane8 >= 72, pltpu.roll(m1, 8, 1), second)
    second = jnp.where(lane8 >= 80, pltpu.roll(m2, 16, 1), second)
    coarse_buf[0, 8:16] = jnp.where(lane8 >= 88, 0.0, second)
    coarse_buf[0, 16:17] = ids

    flat = partner_v[...] - (2 * me - 1) * DOFS
    mate_block = flat // LANES
    mate_lane = flat % LANES

    def jumped(extended):
        out = []
        for s in range(2):
            columns = []
            for t in range(4):
                at = slice(t * LANES, (t + 1) * LANES)
                lanes = jnp.broadcast_to(mate_lane[s : s + 1, at], (CASES, LANES))
                block = jnp.broadcast_to(mate_block[s : s + 1, at], (CASES, LANES))
                mate = jnp.zeros((CASES, LANES), F32)
                for b in range(4 * s, 4 * s + 12):
                    source = extended[b // 4][:, b % 4 * LANES : (b % 4 + 1) * LANES]
                    mate = jnp.where(block == b, take_lanes(source, lanes), mate)
                columns.append(extended[s + 1][:, at] - mate)
            out.append(jnp.concatenate(columns, axis=1))
        return out

    def corner_rows(pair):
        tiles = []
        for s in range(2):
            high, low = split(pair[s])
            both = jnp.concatenate([high] * 8 + [low] * 8, axis=0)
            at = slice(32 * (s + 1), 32 * (s + 2))
            maps = jnp.concatenate([map_high[at], map_low[at]], axis=0)
            product = lax.dot_general(
                maps, both, (((1,), (1,)), ((), ())), preferred_element_type=F32
            )
            rows = product[0:32] + product[32:64]
            rows = rows[:, 0:LANES] + rows[:, LANES : 2 * LANES]
            for k in range(3):
                kept = jnp.where(lane8 // 16 == row8, rows[8 * k : 8 * k + 8], 0.0)
                tiles.append(jnp.sum(kept, axis=0, keepdims=True))
        out = jnp.zeros((8, LANES), F32)
        for r in range(6):
            out = jnp.where(row8 == r, tiles[r], out)
        return out

    def products(pair, other):
        total = jnp.zeros((CASES, LANES), F32)
        for s in range(2):
            product = pair[s] * other[s]
            for t in range(4):
                total = total + product[:, t * LANES : (t + 1) * LANES]
        return jnp.sum(total, axis=1, keepdims=True)

    def as_row(column, place):
        kept = jnp.where(lane16 == row16 + 16 * place, column, 0.0)
        return jnp.sum(kept, axis=0, keepdims=True)

    def as_column(row, place):
        spread = jnp.broadcast_to(row, (CASES, LANES))
        kept = jnp.where(lane16 == row16 + 16 * place, spread, 0.0)
        return jnp.sum(kept, axis=1, keepdims=True)

    def times(parts, v, s):
        top, rest = split(v)
        both = jnp.concatenate([top, rest], axis=0)
        product = dot(jnp.concatenate([both, both], axis=1), parts[s])
        return product[0:CASES] + product[CASES : 2 * CASES]

    def cut(source, parts):
        for s in range(2):

            @pl.loop(0, 8)
            def _(i):
                at = pl.multiple_of(i * 64, 64)
                top, rest = split(source[s, pl.ds(at, 64)])
                parts[s, pl.ds(at, 64)] = top
                parts[s, pl.ds(at + DOFS, 64)] = rest

    def halo_copies(n):
        make = functools.partial(pltpu.make_async_remote_copy, device_id_type=MESH)
        return (
            make(src_ref=field.at[n, 1], dst_ref=halo.at[n, 0], send_sem=halo_send.at[n, 0],
                 recv_sem=halo_recv.at[n, 0], device_id=(right,)),
            make(src_ref=field.at[n, 0], dst_ref=halo.at[n, 1], send_sem=halo_send.at[n, 1],
                 recv_sem=halo_recv.at[n, 1], device_id=(left,)),
        )

    def send_halo(n, pair):
        field[n, 0] = pair[0]
        field[n, 1] = pair[1]
        for copy in halo_copies(n):
            copy.start()

    def extended(n):
        for copy in halo_copies(n):
            copy.wait()
        return [halo[n, 0], field[n, 0], field[n, 1], halo[n, 1]]

    def to_all(buf, rows, n):
        part = pl.ds(0, rows)
        for to, o, c in SENDS:
            pltpu.make_async_remote_copy(
                src_ref=buf.at[0, part], dst_ref=buf.at[to, part], send_sem=all_send.at[n],
                recv_sem=(near_recv if to < NEAR else far_recv).at[n],
                device_id=device(o, c), device_id_type=MESH,
            ).start()

    def forward(buf, rows, n):
        return pltpu.make_async_remote_copy(
            src_ref=buf.at[pl.ds(0, NEAR), pl.ds(0, rows)],
            dst_ref=buf.at[pl.ds(64, NEAR), pl.ds(0, rows)],
            send_sem=fwd_send.at[n], recv_sem=fwd_recv.at[n],
            device_id=device((0, 0, 0), 1), device_id_type=MESH,
        )

    def pass_on(buf, rows, n):
        await_bytes(buf.at[pl.ds(0, len(NEAR_SENDS)), pl.ds(0, rows)], near_recv.at[n])
        forward(buf, rows, n).start()

    def from_all(buf, rows, n):
        await_bytes(buf.at[pl.ds(0, len(FAR_SENDS)), pl.ds(0, rows)], far_recv.at[n])
        await_bytes(buf.at[pl.ds(0, len(SENDS)), pl.ds(0, rows)], all_send.at[n])
        forward(buf, rows, n).wait()

    load = [load_v[:, s, :] for s in range(2)]
    buf1[0] = corner_rows(load)
    copies[5].wait()
    cut(inverse_v, inverse_parts)
    solved_load = [times(inverse_parts, load[s], s) for s in range(2)]

    pl.semaphore_wait(barrier, 127)
    to_all(coarse_buf, 17, 0)
    to_all(buf1, 6, 1)
    side_copies = []
    for i, (dev, near) in enumerate(((right, 1), (left, 0))):
        for n, (src, dst) in enumerate(
            ((map_v.at[near], map_side.at[i]), (coarse_buf.at[0, pl.ds(16, 1)], id_side.at[i]))
        ):
            side_copies.append(
                pltpu.make_async_remote_copy(
                    src_ref=src, dst_ref=dst, send_sem=halo_send.at[5 + n, i],
                    recv_sem=halo_recv.at[5 + n, i], device_id=(dev,), device_id_type=MESH,
                )
            )
    for copy in side_copies:
        copy.start()
    send_halo(0, solved_load)
    copies[6].wait()
    cut(schur_v, schur_parts)
    for copy in side_copies:
        copy.wait()
    for i in range(2):
        high, low = split(jnp.concatenate([map_side[i], gap], axis=0))
        map_high[96 * i : 96 * i + 32] = high
        map_low[96 * i : 96 * i + 32] = low
    row48 = iota((48, LANES), 0)
    lane48 = iota((48, LANES), 1)

    def id_column(row):
        kept = jnp.where(row48 == lane48, jnp.broadcast_to(row, (48, LANES)), 0.0)
        return jnp.sum(kept, axis=1, keepdims=True)

    corner = jnp.concatenate(
        [id_column(id_side[0])[24:48], id_column(ids), id_column(id_side[1])[0:24]], axis=0
    ).astype(I32)
    owner = corner // OWN
    inner = corner - owner * OWN
    third = inner // 8
    pass_on(coarse_buf, 17, 0)
    pass_on(buf1, 6, 1)
    from_all(coarse_buf, 17, 0)

    id_lanes = jnp.transpose(coarse_buf[:, 16, :])
    id_rows[...] = id_lanes[0:48].astype(I32)
    owned = jnp.where(id_lanes[48:49].astype(I32) == owner, 1.0, 0.0)
    wanted = jnp.concatenate([inner % 8 + jnp.where(third == 2, 8, 0), 8 + inner % 8], axis=0)
    owned = jnp.concatenate([owned, owned], axis=0)
    pick = jnp.concatenate(
        [jnp.where(wanted == r, owned, 0.0).astype(BF16) for r in range(16)], axis=1
    )
    high, low = split(jnp.concatenate([coarse_buf[:, r, :] for r in range(16)], axis=0))
    found = dot(pick, jnp.concatenate([high, low], axis=1))
    found = found[:, 0:LANES] + found[:, LANES : 2 * LANES]
    lane96 = iota((96, LANES), 1)
    from_a = take_lanes(found[0:96], jnp.minimum(lane96 + jnp.where(third == 1, 64, 0), LANES - 1))
    from_t = take_lanes(found[96:192], jnp.minimum(lane96 + 8 * third, LANES - 1))
    table[...] = jnp.where(lane96 < 64, from_a, jnp.where(lane96 < WIN, from_t, 0.0))
    bases[...] = jnp.broadcast_to((owner - 1) * OWN, (96, LANES))

    @pl.loop(0, 8)
    def _(e):
        everyone = [id_rows[pl.ds(8 * r + e, 1), :] for r in range(6)]
        for k in range(6):
            rows = table[16 * k : 16 * k + 16]
            base = bases[16 * k : 16 * k + 16]
            out = pl.ds(pl.multiple_of(e * 96 + k * 16, 16), 16)
            for r in range(6):
                place = jnp.broadcast_to(everyone[r], (16, LANES)) - base
                place = jnp.where((place < 0) | (place >= WIN), LANES - 1, place)
                top, rest = split(take_lanes(rows, place))
                operator[out, r * LANES : (r + 1) * LANES] = top
                operator[out, (r + 6) * LANES : (r + 7) * LANES] = rest

    from_all(buf1, 6, 1)

    def spread(buf):
        top, rest = split(jnp.concatenate([buf[:, r, :] for r in range(6)], axis=0))
        both = jnp.concatenate([top, rest], axis=1)
        product = dot(operator[...], jnp.concatenate([both, both], axis=0))
        solved = jnp.zeros((96, 2 * LANES), F32)
        lanes = iota((96, 2 * LANES), 1) % LANES // 16
        for e in range(8):
            solved = jnp.where(lanes == e, product[96 * e : 96 * e + 96], solved)
        solved = solved[:, 0:LANES] + solved[:, LANES : 2 * LANES]
        zero = jnp.zeros((8, LANES), F32)
        padded = []
        for j in range(4):
            padded += [solved[24 * j : 24 * j + 24], zero]
        turned = jnp.transpose(jnp.concatenate(padded, axis=0))
        by_case = turned[0:CASES]
        for e in range(1, 8):
            by_case = by_case + turned[CASES * e : CASES * e + CASES]
        stack = []
        for j in range(4):
            stack += list(split(jnp.where(lane16 // 32 == j, by_case, 0.0)))
        stack = jnp.concatenate(stack, axis=0)
        product = dot(stack, map_high[...]) + dot(stack, map_low[...])
        return [product[32 * j : 32 * j + 16] + product[32 * j + 16 : 32 * j + 32] for j in range(4)]

    def add(first, second):
        return [a + b for a, b in zip(first, second)]

    def precondition(n, pair):
        send_halo(n, [times(schur_parts, pair[s], s) for s in range(2)])
        return [0.5 * v for v in jumped(extended(n))]

    r0 = jumped(add(spread(buf1), extended(0)))
    a = precondition(1, r0)

    buf2[0] = corner_rows(a)
    to_all(buf2, 6, 2)
    send_halo(2, [times(inverse_parts, a[s], s) for s in range(2)])
    pass_on(buf2, 6, 2)
    solved_a = extended(2)
    from_all(buf2, 6, 2)

    q = [2.0 * v for v in jumped(add(spread(buf2), solved_a))]
    send_halo(3, [times(schur_parts, q[s], s) for s in range(2)])
    dots = as_row(products(r0, a), 0) + as_row(products(a, q), 1)
    w = [0.5 * v for v in jumped(extended(3))]

    buf3[0] = jnp.where(row8 == 6, dots, corner_rows(w))
    to_all(buf3, 7, 3)
    send_halo(4, [times(inverse_parts, w[s], s) for s in range(2)])
    pass_on(buf3, 7, 3)
    solved_w = extended(4)
    from_all(buf3, 7, 3)

    u = [2.0 * v for v in jumped(add(spread(buf3), solved_w))]
    total = jnp.sum(buf3[:, 6, :], axis=0, keepdims=True)
    current, curvature = as_column(total, 0), as_column(total, 1)
    step0 = current / curvature
    r1 = [r0[s] - step0 * q[s] for s in range(2)]
    z1 = [a[s] - step0 * w[s] for s in range(2)]
    image = [q[s] - step0 * u[s] for s in range(2)]
    cross = products(z1, q) + products(a, image)
    dots = as_row(products(r1, z1), 0) + as_row(products(z1, image), 1) + as_row(cross, 2)
    buf4[0] = jnp.where(row8 == 0, dots, 0.0)
    for to, o, c in EVERYONE:
        pltpu.make_async_remote_copy(
            src_ref=buf4.at[0, pl.ds(0, 1)], dst_ref=buf4.at[to, pl.ds(0, 1)],
            send_sem=all_send.at[4], recv_sem=far_recv.at[4],
            device_id=device(o, c), device_id_type=MESH,
        ).start()
    await_bytes(buf4.at[pl.ds(0, 127), pl.ds(0, 1)], far_recv.at[4])
    total = jnp.sum(buf4[:, 0, :], axis=0, keepdims=True)
    following = as_column(total, 0)
    ratio = following / current
    curvature1 = as_column(total, 1) + ratio * as_column(total, 2) + ratio * ratio * curvature
    step1 = following / curvature1
    for s in range(2):
        mult_ref[:, s, :] = step0 * a[s] + step1 * (z1[s] + ratio * a[s])
        resid_ref[:, s, :] = r1[s] - step1 * (image[s] + ratio * q[s])

    await_bytes(buf4.at[pl.ds(0, 127), pl.ds(0, 1)], all_send.at[4])


def per_device(load, schur_inverse, schur, corner_map, corner_ids, coarse_inverse, partner):
    vmem = pltpu.VMEM
    dma = pltpu.SemaphoreType.DMA
    out = jax.ShapeDtypeStruct(load.shape, F32)
    inputs = (load, schur_inverse, schur, corner_map, corner_ids, coarse_inverse, partner)
    parts = vmem((2, 2 * DOFS, DOFS), BF16)
    slots = vmem((128, 8, LANES), F32)
    return pl.pallas_call(
        kernel,
        out_shape=(out, out),
        in_specs=[pl.BlockSpec(memory_space=pltpu.HBM)] * 7,
        out_specs=(pl.BlockSpec(memory_space=vmem),) * 2,
        scratch_shapes=[
            *(vmem(v.shape, v.dtype) for v in inputs),
            parts, parts,
            vmem((128, DOFS), BF16), vmem((128, DOFS), BF16),
            vmem((2, CORNERS, DOFS), F32), vmem((2, 1, LANES), F32),
            vmem((96, LANES), F32), vmem((96, LANES), I32), vmem((48, LANES), I32),
            vmem((768, 1536), BF16),
            vmem((5, 2, CASES, DOFS), F32), vmem((5, 2, CASES, DOFS), F32),
            vmem((128, 24, LANES), F32), slots, slots, slots, slots,
            dma((7,)), dma((5,)), dma((5,)), dma((5,)), dma((4,)), dma((4,)),
            dma((7, 2)), dma((7, 2)),
        ],
        compiler_params=pltpu.CompilerParams(
            collective_id=0, has_side_effects=True, vmem_limit_bytes=63 << 20
        ),
    )(*inputs)


def solution(mesh):
    in_specs = (
        P(None, "sub", None),
        P("sub", None, None),
        P("sub", None, None),
        P("sub", None, None),
        P("sub", None),
        P("sub", None),
        P("sub", None),
    )
    out_specs = (P(None, "sub", None), P(None, "sub", None))
    return jax.shard_map(
        per_device, mesh=mesh, in_specs=in_specs, out_specs=out_specs, check_vma=False
    )
```

```python
import functools
import itertools

import jax
import jax.numpy as jnp
from jax import lax
from jax.experimental import pallas as pl
from jax.experimental.pallas import tpu as pltpu
from jax.sharding import PartitionSpec as P

MESH = pl.DeviceIdType.MESH
F32, BF16, I32 = jnp.float32, jnp.bfloat16, jnp.int32
CASES, DOFS, CORNERS, OWN, WIN = 16, 512, 24, 24, 72
LANES = 128
HOPS = (0, 1, 2, 1)

CHIPS = sorted(
    itertools.product(range(4), repeat=3), key=lambda o: -sum(HOPS[d] for d in o)
)
ROUTES = ((2, 1, 0), (1, 0, 2), (0, 2, 1))


def place_of(o):
    return sum(o[axis] * 4**k for k, axis in enumerate(ROUTES[2]))


def split(v):
    high = v.astype(BF16)
    return high, (v - high.astype(F32)).astype(BF16)


def await_bytes(ref, sem):
    pltpu.make_async_copy(ref, ref, sem).wait()


def dot(a, b):
    return jnp.dot(a, b, preferred_element_type=F32)


def take_lanes(values, lanes):
    return jnp.take_along_axis(values, lanes, axis=1, mode="promise_in_bounds")


def iota(shape, dim):
    return lax.broadcasted_iota(I32, shape, dim)


def kernel(
    load_hbm, inverse_hbm, schur_hbm, map_hbm, ids_hbm, coarse_hbm, partner_hbm,
    mult_ref, resid_ref,
    load_v, inverse_v, schur_v, map_v, ids_v, coarse_v, partner_v,
    inverse_parts, schur_parts, map_high, map_low, map_side, id_side,
    table, bases, id_rows, operator, field, halo, coarse_a, coarse_b, buf1, buf2, buf3, buf4,
    in_sem, stage_send, stage_recv, all_send, all_recv, fwd_send, fwd_recv, halo_send, halo_recv,
):
    me = lax.axis_index("sub")
    core, chip = me % 2, me // 2
    y, x, z = chip % 4, chip // 4 % 4, chip // 16
    zs = [(z + i) % 4 * 32 for i in range(4)]
    xs = [(x + i) % 4 * 8 for i in range(4)]
    ys = [(y + i) % 4 * 2 for i in range(4)]
    cs = [core, 1 - core]
    right, left = (me + 1) % 128, (me + 127) % 128

    def device(o, c):
        return (zs[o[0]] + xs[o[1]] + ys[o[2]] + cs[c],)

    def steps(axis, k):
        return tuple(k if i == axis else 0 for i in range(3))

    pairs = (
        (map_hbm, map_v), (load_hbm, load_v), (ids_hbm, ids_v), (coarse_hbm, coarse_v),
        (partner_hbm, partner_v), (inverse_hbm, inverse_v), (schur_hbm, schur_v),
    )
    copies = [pltpu.make_async_copy(a, b, in_sem.at[i]) for i, (a, b) in enumerate(pairs)]
    for copy in copies:
        copy.start()

    barrier = pltpu.get_barrier_semaphore()
    partners = [device(steps(axis, k), 0) for axis in range(3) for k in (2, 1, 3)]
    partners += [(jnp.where(core == 0, left, right),), device((0, 0, 0), 1)]
    for partner in partners:
        pl.semaphore_signal(barrier, inc=1, device_id=partner, device_id_type=MESH)

    lane8 = iota((8, LANES), 1)
    row8 = iota((8, LANES), 0)
    lane16 = iota((CASES, LANES), 1)
    row16 = iota((CASES, LANES), 0)

    for copy in copies[:5]:
        copy.wait()
    gap = jnp.zeros((8, DOFS), F32)
    own_maps = [map_v[s] for s in range(2)]
    for s in range(2):
        high, low = split(jnp.concatenate([own_maps[s], gap], axis=0))
        map_high[32 * (s + 1) : 32 * (s + 2)] = high
        map_low[32 * (s + 1) : 32 * (s + 2)] = low

    coarse = jnp.concatenate([coarse_v[...], jnp.zeros((OWN, LANES - WIN), F32)], axis=1)
    m0, m1, m2 = coarse[0:8], coarse[8:16], coarse[16:24]
    ids = jnp.concatenate([ids_v[...].astype(F32), jnp.zeros((2, LANES - CORNERS), F32)], axis=1)
    ids = jnp.where(lane8[0:1] < CORNERS, ids[0:1], pltpu.roll(ids, CORNERS, 1)[1:2])
    coarse_a[0] = jnp.where(lane8 < 64, m0, pltpu.roll(m1, 64, 1))
    second = jnp.where(lane8 < 64, m2, m0)
    second = jnp.where(lane8 >= 72, pltpu.roll(m1, 8, 1), second)
    second = jnp.where(lane8 >= 80, pltpu.roll(m2, 16, 1), second)
    coarse_b[0] = jnp.where(lane8 >= 88, 0.0, second)

    flat = partner_v[...] - (2 * me - 1) * DOFS
    mate_block = flat // LANES
    mate_lane = flat % LANES

    def jumped(extended):
        out = []
        for s in range(2):
            columns = []
            for t in range(4):
                at = slice(t * LANES, (t + 1) * LANES)
                lanes = jnp.broadcast_to(mate_lane[s : s + 1, at], (CASES, LANES))
                block = jnp.broadcast_to(mate_block[s : s + 1, at], (CASES, LANES))
                mate = jnp.zeros((CASES, LANES), F32)
                for b in range(4 * s, 4 * s + 12):
                    source = extended[b // 4][:, b % 4 * LANES : (b % 4 + 1) * LANES]
                    mate = jnp.where(block == b, take_lanes(source, lanes), mate)
                columns.append(extended[s + 1][:, at] - mate)
            out.append(jnp.concatenate(columns, axis=1))
        return out

    def corner_rows(pair):
        tiles = []
        for s in range(2):
            high, low = split(pair[s])
            both = jnp.concatenate([high] * 8 + [low] * 8, axis=0)
            at = slice(32 * (s + 1), 32 * (s + 2))
            maps = jnp.concatenate([map_high[at], map_low[at]], axis=0)
            product = lax.dot_general(
                maps, both, (((1,), (1,)), ((), ())), preferred_element_type=F32
            )
            rows = product[0:32] + product[32:64]
            rows = rows[:, 0:LANES] + rows[:, LANES : 2 * LANES]
            for k in range(3):
                kept = jnp.where(lane8 // 16 == row8, rows[8 * k : 8 * k + 8], 0.0)
                tiles.append(jnp.sum(kept, axis=0, keepdims=True))
        out = jnp.zeros((8, LANES), F32)
        for r in range(6):
            out = jnp.where(row8 == r, tiles[r], out)
        return out

    def products(pair, other):
        total = jnp.zeros((CASES, LANES), F32)
        for s in range(2):
            product = pair[s] * other[s]
            for t in range(4):
                total = total + product[:, t * LANES : (t + 1) * LANES]
        return jnp.sum(total, axis=1, keepdims=True)

    def as_row(column, place):
        kept = jnp.where(lane16 == row16 + 16 * place, column, 0.0)
        return jnp.sum(kept, axis=0, keepdims=True)

    def as_column(row, place):
        spread = jnp.broadcast_to(row, (CASES, LANES))
        kept = jnp.where(lane16 == row16 + 16 * place, spread, 0.0)
        return jnp.sum(kept, axis=1, keepdims=True)

    def times(parts, v, s):
        top, rest = split(v)
        both = jnp.concatenate([top, rest], axis=0)
        product = dot(jnp.concatenate([both, both], axis=1), parts[s])
        return product[0:CASES] + product[CASES : 2 * CASES]

    def cut(source, parts):
        for s in range(2):

            @pl.loop(0, 8)
            def _(i):
                at = pl.multiple_of(i * 64, 64)
                top, rest = split(source[s, pl.ds(at, 64)])
                parts[s, pl.ds(at, 64)] = top
                parts[s, pl.ds(at + DOFS, 64)] = rest

    def halo_copies(n):
        make = functools.partial(pltpu.make_async_remote_copy, device_id_type=MESH)
        return (
            make(src_ref=field.at[n, 1], dst_ref=halo.at[n, 0], send_sem=halo_send.at[n, 0],
                 recv_sem=halo_recv.at[n, 0], device_id=(right,)),
            make(src_ref=field.at[n, 0], dst_ref=halo.at[n, 1], send_sem=halo_send.at[n, 1],
                 recv_sem=halo_recv.at[n, 1], device_id=(left,)),
        )

    def send_halo(n, pair):
        field[n, 0] = pair[0]
        field[n, 1] = pair[1]
        for copy in halo_copies(n):
            copy.start()

    def extended(n):
        for copy in halo_copies(n):
            copy.wait()
        return [halo[n, 0], field[n, 0], field[n, 1], halo[n, 1]]

    def to_all(buf, rows, n):
        part = pl.ds(0, rows)
        for o in CHIPS[:-1]:
            pltpu.make_async_remote_copy(
                src_ref=buf.at[0, part], dst_ref=buf.at[place_of(o), part],
                send_sem=all_send.at[n], recv_sem=all_recv.at[n],
                device_id=device(o, 0), device_id_type=MESH,
            ).start()

    def forward(buf, rows, n):
        return pltpu.make_async_remote_copy(
            src_ref=buf.at[pl.ds(0, 64), pl.ds(0, rows)],
            dst_ref=buf.at[pl.ds(64, 64), pl.ds(0, rows)],
            send_sem=fwd_send.at[n], recv_sem=fwd_recv.at[n],
            device_id=device((0, 0, 0), 1), device_id_type=MESH,
        )

    def from_all(buf, rows, n):
        others = buf.at[pl.ds(0, 63), pl.ds(0, rows)]
        await_bytes(others, all_recv.at[n])
        copy = forward(buf, rows, n)
        copy.start()
        await_bytes(others, all_send.at[n])
        copy.wait()

    thirds = (coarse_a, coarse_b, buf1)

    def send_stage(third, stage):
        buf, axis, size = thirds[third], ROUTES[third][stage], 4**stage
        for k in (2, 1, 3):
            pltpu.make_async_remote_copy(
                src_ref=buf.at[pl.ds(0, size)], dst_ref=buf.at[pl.ds(k * size, size)],
                send_sem=stage_send.at[third, stage], recv_sem=stage_recv.at[third, stage],
                device_id=device(steps(axis, k), 0), device_id_type=MESH,
            ).start()

    def await_stage(sems, third, stage):
        await_bytes(thirds[third].at[pl.ds(0, 3 * 4**stage)], sems.at[third, stage])

    load = [load_v[:, s, :] for s in range(2)]
    buf1[0] = jnp.where(row8 == 6, ids, corner_rows(load))

    pl.semaphore_wait(barrier, len(partners))
    for third in range(3):
        send_stage(third, 0)
    side_copies = []
    for i, (dev, near) in enumerate(((right, 1), (left, 0))):
        for n, (src, dst) in enumerate(
            ((map_v.at[near], map_side.at[i]), (buf1.at[0, pl.ds(6, 1)], id_side.at[i]))
        ):
            side_copies.append(
                pltpu.make_async_remote_copy(
                    src_ref=src, dst_ref=dst, send_sem=halo_send.at[5 + n, i],
                    recv_sem=halo_recv.at[5 + n, i], device_id=(dev,), device_id_type=MESH,
                )
            )
    for copy in side_copies:
        copy.start()
    copies[5].wait()
    cut(inverse_v, inverse_parts)
    for third in range(3):
        await_stage(stage_recv, third, 0)
        send_stage(third, 1)
    send_halo(0, [times(inverse_parts, load[s], s) for s in range(2)])
    for third in range(3):
        await_stage(stage_recv, third, 1)
        send_stage(third, 2)
    copies[6].wait()
    cut(schur_v, schur_parts)
    for copy in side_copies:
        copy.wait()
    for i in range(2):
        high, low = split(jnp.concatenate([map_side[i], gap], axis=0))
        map_high[96 * i : 96 * i + 32] = high
        map_low[96 * i : 96 * i + 32] = low
    row48 = iota((48, LANES), 0)
    lane48 = iota((48, LANES), 1)

    def id_column(row):
        kept = jnp.where(row48 == lane48, jnp.broadcast_to(row, (48, LANES)), 0.0)
        return jnp.sum(kept, axis=1, keepdims=True)

    corner = jnp.concatenate(
        [id_column(id_side[0])[24:48], id_column(ids), id_column(id_side[1])[0:24]], axis=0
    ).astype(I32)
    owner = corner // OWN
    inner = corner - owner * OWN
    third_of = inner // 8
    wanted = jnp.concatenate(
        [inner % 8 + jnp.where(third_of == 2, 8, 0), 8 + inner % 8], axis=0
    )
    slots = iota((1, LANES), 1)

    def owned(third):
        digits = [slots // 4**k % 4 for k in range(3)]
        dz, dx, dy = (digits[ROUTES[third].index(axis)] for axis in range(3))
        held = (z - dz) % 4 * 32 + (x - dx) % 4 * 8 + (y - dy) % 4 * 2 + (core + slots // 64) % 2
        one = jnp.where(held == owner, 1.0, 0.0)
        return jnp.concatenate([one, one], axis=0)

    pick = jnp.concatenate(
        [jnp.where(wanted == 8 * t + r, owned(t), 0.0).astype(BF16) for t in range(2) for r in range(8)],
        axis=1,
    )
    for third in range(3):
        await_stage(stage_recv, third, 2)
        forward(thirds[third], 8, third).start()
    for third in range(3):
        forward(thirds[third], 8, third).wait()
        for stage in range(3):
            await_stage(stage_send, third, stage)

    id_rows[...] = jnp.transpose(buf1[:, 6, :])[0:48].astype(I32)
    packed = [buf[:, r, :] for buf in (coarse_a, coarse_b) for r in range(8)]
    high, low = split(jnp.concatenate(packed, axis=0))
    found = dot(pick, jnp.concatenate([high, low], axis=1))
    found = found[:, 0:LANES] + found[:, LANES : 2 * LANES]
    at = iota((96, LANES), 1) - 1
    from_a = take_lanes(found[0:96], jnp.clip(at + jnp.where(third_of == 1, 64, 0), 0, LANES - 1))
    from_t = take_lanes(found[96:192], jnp.clip(at + 8 * third_of, 0, LANES - 1))
    window = jnp.where(at < 64, from_a, from_t)
    table[...] = jnp.where((at >= 0) & (at < WIN), window, 0.0)
    bases[...] = jnp.broadcast_to((owner - 1) * OWN - 1, (96, LANES))

    @pl.loop(0, 8)
    def _(e):
        everyone = [id_rows[pl.ds(8 * r + e, 1), :] for r in range(6)]
        for k in range(6):
            rows = table[16 * k : 16 * k + 16]
            base = bases[16 * k : 16 * k + 16]
            out = pl.ds(pl.multiple_of(e * 96 + k * 16, 16), 16)
            for r in range(6):
                place = jnp.broadcast_to(everyone[r], (16, LANES)) - base
                top, rest = split(take_lanes(rows, jnp.clip(place, 0, LANES - 1)))
                operator[out, r * LANES : (r + 1) * LANES] = top
                operator[out, (r + 6) * LANES : (r + 7) * LANES] = rest

    def spread(buf):
        top, rest = split(jnp.concatenate([buf[:, r, :] for r in range(6)], axis=0))
        both = jnp.concatenate([top, rest], axis=1)
        product = dot(operator[...], jnp.concatenate([both, both], axis=0))
        solved = jnp.zeros((96, 2 * LANES), F32)
        lanes = iota((96, 2 * LANES), 1) % LANES // 16
        for e in range(8):
            solved = jnp.where(lanes == e, product[96 * e : 96 * e + 96], solved)
        solved = solved[:, 0:LANES] + solved[:, LANES : 2 * LANES]
        zero = jnp.zeros((8, LANES), F32)
        padded = []
        for j in range(4):
            padded += [solved[24 * j : 24 * j + 24], zero]
        turned = jnp.transpose(jnp.concatenate(padded, axis=0))
        by_case = turned[0:CASES]
        for e in range(1, 8):
            by_case = by_case + turned[CASES * e : CASES * e + CASES]
        stack = []
        for j in range(4):
            stack += list(split(jnp.where(lane16 // 32 == j, by_case, 0.0)))
        stack = jnp.concatenate(stack, axis=0)
        product = dot(stack, map_high[...]) + dot(stack, map_low[...])
        return [product[32 * j : 32 * j + 16] + product[32 * j + 16 : 32 * j + 32] for j in range(4)]

    def add(first, second):
        return [a + b for a, b in zip(first, second)]

    def precondition(n, pair):
        send_halo(n, [times(schur_parts, pair[s], s) for s in range(2)])
        return [0.5 * v for v in jumped(extended(n))]

    r0 = jumped(add(spread(buf1), extended(0)))
    a = precondition(1, r0)

    buf2[0] = corner_rows(a)
    to_all(buf2, 6, 3)
    send_halo(2, [times(inverse_parts, a[s], s) for s in range(2)])
    solved_a = extended(2)
    from_all(buf2, 6, 3)

    s_a = add(spread(buf2), solved_a)
    q = [2.0 * v for v in jumped(s_a)]
    send_halo(3, [times(schur_parts, q[s], s) for s in range(2)])
    dots = as_row(products(r0, a), 0) + as_row(products(a, q), 1)
    w = [0.5 * v for v in jumped(extended(3))]

    buf3[0] = jnp.where(row8 == 6, dots, corner_rows(w))
    to_all(buf3, 7, 4)
    send_halo(4, [times(inverse_parts, w[s], s) for s in range(2)])
    solved_w = extended(4)
    from_all(buf3, 7, 4)

    s_w = add(spread(buf3), solved_w)
    total = jnp.sum(buf3[:, 6, :], axis=0, keepdims=True)
    current, curvature = as_column(total, 0), as_column(total, 1)
    step0 = current / curvature
    r1 = [r0[s] - step0 * q[s] for s in range(2)]
    z1 = [a[s] - step0 * w[s] for s in range(2)]
    s_z = [s_a[s + 1] - step0 * s_w[s + 1] for s in range(2)]
    cross = 4.0 * (products(z1, s_a[1:3]) + products(a, s_z))
    dots = as_row(products(r1, z1), 0) + as_row(4.0 * products(z1, s_z), 1) + as_row(cross, 2)
    buf4[0] = jnp.where(row8 == 0, dots, 0.0)
    for o in CHIPS:
        for c in range(2):
            if place_of(o) + c > 0:
                pltpu.make_async_remote_copy(
                    src_ref=buf4.at[0, pl.ds(0, 1)],
                    dst_ref=buf4.at[place_of(o) + 64 * c, pl.ds(0, 1)],
                    send_sem=all_send.at[5], recv_sem=all_recv.at[5],
                    device_id=device(o, c), device_id_type=MESH,
                ).start()
    u = [2.0 * v for v in jumped(s_w)]
    image = [q[s] - step0 * u[s] for s in range(2)]
    await_bytes(buf4.at[pl.ds(0, 127), pl.ds(0, 1)], all_recv.at[5])
    total = jnp.sum(buf4[:, 0, :], axis=0, keepdims=True)
    following = as_column(total, 0)
    ratio = following / current
    curvature1 = as_column(total, 1) + ratio * as_column(total, 2) + ratio * ratio * curvature
    step1 = following / curvature1
    for s in range(2):
        mult_ref[:, s, :] = step0 * a[s] + step1 * (z1[s] + ratio * a[s])
        resid_ref[:, s, :] = r1[s] - step1 * (image[s] + ratio * q[s])

    await_bytes(buf4.at[pl.ds(0, 127), pl.ds(0, 1)], all_send.at[5])


def per_device(load, schur_inverse, schur, corner_map, corner_ids, coarse_inverse, partner):
    vmem = pltpu.VMEM
    dma = pltpu.SemaphoreType.DMA
    out = jax.ShapeDtypeStruct(load.shape, F32)
    inputs = (load, schur_inverse, schur, corner_map, corner_ids, coarse_inverse, partner)
    parts = vmem((2, 2 * DOFS, DOFS), BF16)
    slots = vmem((128, 8, LANES), F32)
    return pl.pallas_call(
        kernel,
        out_shape=(out, out),
        in_specs=[pl.BlockSpec(memory_space=pltpu.HBM)] * 7,
        out_specs=(pl.BlockSpec(memory_space=vmem),) * 2,
        scratch_shapes=[
            *(vmem(v.shape, v.dtype) for v in inputs),
            parts, parts,
            vmem((128, DOFS), BF16), vmem((128, DOFS), BF16),
            vmem((2, CORNERS, DOFS), F32), vmem((2, 1, LANES), F32),
            vmem((96, LANES), F32), vmem((96, LANES), I32), vmem((48, LANES), I32),
            vmem((768, 1536), BF16),
            vmem((5, 2, CASES, DOFS), F32), vmem((5, 2, CASES, DOFS), F32),
            slots, slots, slots, slots, slots, slots,
            dma((7,)), dma((3, 3)), dma((3, 3)), dma((6,)), dma((6,)), dma((5,)), dma((5,)),
            dma((7, 2)), dma((7, 2)),
        ],
        compiler_params=pltpu.CompilerParams(
            collective_id=0, has_side_effects=True, vmem_limit_bytes=63 << 20
        ),
    )(*inputs)


def solution(mesh):
    in_specs = (
        P(None, "sub", None),
        P("sub", None, None),
        P("sub", None, None),
        P("sub", None, None),
        P("sub", None),
        P("sub", None),
        P("sub", None),
    )
    out_specs = (P(None, "sub", None), P(None, "sub", None))
    return jax.shard_map(
        per_device, mesh=mesh, in_specs=in_specs, out_specs=out_specs, check_vma=False
    )
```

```python
import functools
import itertools

import jax
import jax.numpy as jnp
from jax import lax
from jax.experimental import pallas as pl
from jax.experimental.pallas import tpu as pltpu
from jax.sharding import PartitionSpec as P

MESH = pl.DeviceIdType.MESH
F32, BF16, I32 = jnp.float32, jnp.bfloat16, jnp.int32
CASES, DOFS, CORNERS, OWN, WIN = 16, 512, 24, 24, 72
LANES = 128
HOPS = (0, 1, 2, 1)

CHIPS = sorted(
    itertools.product(range(4), repeat=3), key=lambda o: -sum(HOPS[d] for d in o)
)
ROUTES = ((2, 1, 0), (1, 0, 2), (0, 2, 1))


def place_of(o):
    return sum(o[axis] * 4**k for k, axis in enumerate(ROUTES[2]))


def split(v):
    high = v.astype(BF16)
    return high, (v - high.astype(F32)).astype(BF16)


def await_bytes(ref, sem):
    pltpu.make_async_copy(ref, ref, sem).wait()


def dot(a, b):
    return jnp.dot(a, b, preferred_element_type=F32)


def take_lanes(values, lanes):
    return jnp.take_along_axis(values, lanes, axis=1, mode="promise_in_bounds")


def iota(shape, dim):
    return lax.broadcasted_iota(I32, shape, dim)


def kernel(
    load_hbm, inverse_hbm, schur_hbm, map_hbm, ids_hbm, coarse_hbm, partner_hbm,
    mult_ref, resid_ref,
    load_v, inverse_v, schur_v, map_v, ids_v, coarse_v, partner_v,
    inverse_parts, schur_parts, map_high, map_low, map_side, id_side,
    partner_side, schur_side, side_parts, table, bases, id_rows, operator, operator_wide,
    field, halo, halo_wide, coarse_a, coarse_b, buf1, buf2, buf3, buf4,
    in_sem, stage_send, stage_recv, all_send, all_recv, fwd_send, fwd_recv, halo_send, halo_recv,
    side_send, side_recv,
):
    me = lax.axis_index("sub")
    core, chip = me % 2, me // 2
    y, x, z = chip % 4, chip // 4 % 4, chip // 16
    zs = [(z + i) % 4 * 32 for i in range(4)]
    xs = [(x + i) % 4 * 8 for i in range(4)]
    ys = [(y + i) % 4 * 2 for i in range(4)]
    cs = [core, 1 - core]
    right, left = (me + 1) % 128, (me + 127) % 128

    def device(o, c):
        return (zs[o[0]] + xs[o[1]] + ys[o[2]] + cs[c],)

    def steps(axis, k):
        return tuple(k if i == axis else 0 for i in range(3))

    pairs = (
        (map_hbm, map_v), (load_hbm, load_v), (ids_hbm, ids_v), (coarse_hbm, coarse_v),
        (partner_hbm, partner_v), (inverse_hbm, inverse_v), (schur_hbm, schur_v),
    )
    copies = [pltpu.make_async_copy(a, b, in_sem.at[i]) for i, (a, b) in enumerate(pairs)]
    for copy in copies:
        copy.start()

    barrier = pltpu.get_barrier_semaphore()
    partners = [device(steps(axis, k), 0) for axis in range(3) for k in (2, 1, 3)]
    partners += [(jnp.where(core == 0, left, right),), device((0, 0, 0), 1)]
    for partner in partners:
        pl.semaphore_signal(barrier, inc=1, device_id=partner, device_id_type=MESH)

    lane8 = iota((8, LANES), 1)
    row8 = iota((8, LANES), 0)
    lane16 = iota((CASES, LANES), 1)
    row16 = iota((CASES, LANES), 0)

    for copy in copies[:5]:
        copy.wait()
    gap = jnp.zeros((8, DOFS), F32)
    map_high[192:256] = jnp.zeros((64, DOFS), BF16)
    map_low[192:256] = jnp.zeros((64, DOFS), BF16)
    own_maps = [map_v[s] for s in range(2)]
    for s in range(2):
        high, low = split(jnp.concatenate([own_maps[s], gap], axis=0))
        map_high[32 * (s + 1) : 32 * (s + 2)] = high
        map_low[32 * (s + 1) : 32 * (s + 2)] = low

    coarse = jnp.concatenate([coarse_v[...], jnp.zeros((OWN, LANES - WIN), F32)], axis=1)
    m0, m1, m2 = coarse[0:8], coarse[8:16], coarse[16:24]
    ids = jnp.concatenate([ids_v[...].astype(F32), jnp.zeros((2, LANES - CORNERS), F32)], axis=1)
    ids = jnp.where(lane8[0:1] < CORNERS, ids[0:1], pltpu.roll(ids, CORNERS, 1)[1:2])
    coarse_a[0] = jnp.where(lane8 < 64, m0, pltpu.roll(m1, 64, 1))
    second = jnp.where(lane8 < 64, m2, m0)
    second = jnp.where(lane8 >= 72, pltpu.roll(m1, 8, 1), second)
    second = jnp.where(lane8 >= 80, pltpu.roll(m2, 16, 1), second)
    coarse_b[0] = jnp.where(lane8 >= 88, 0.0, second)

    def jump(window, partners):
        columns = []
        for t in range(4):
            at = slice(t * LANES, (t + 1) * LANES)
            flat = jnp.broadcast_to(partners[:, at], (CASES, LANES))
            lanes, block = flat % LANES, flat // LANES
            mate = jnp.zeros((CASES, LANES), F32)
            for b in range(12):
                source = window[b // 4][:, b % 4 * LANES : (b % 4 + 1) * LANES]
                mate = jnp.where(block == b, take_lanes(source, lanes), mate)
            columns.append(window[1][:, at] - mate)
        return jnp.concatenate(columns, axis=1)

    own_partners = [partner_v[s : s + 1] - (2 * me + s - 1) * DOFS for s in range(2)]

    def jumped(extended):
        return [jump(extended[s : s + 3], own_partners[s]) for s in range(2)]

    def corner_rows(pair):
        tiles = []
        for s in range(2):
            high, low = split(pair[s])
            both = jnp.concatenate([high] * 8 + [low] * 8, axis=0)
            at = slice(32 * (s + 1), 32 * (s + 2))
            maps = jnp.concatenate([map_high[at], map_low[at]], axis=0)
            product = lax.dot_general(
                maps, both, (((1,), (1,)), ((), ())), preferred_element_type=F32
            )
            rows = product[0:32] + product[32:64]
            rows = rows[:, 0:LANES] + rows[:, LANES : 2 * LANES]
            for k in range(3):
                kept = jnp.where(lane8 // 16 == row8, rows[8 * k : 8 * k + 8], 0.0)
                tiles.append(jnp.sum(kept, axis=0, keepdims=True))
        out = jnp.zeros((8, LANES), F32)
        for r in range(6):
            out = jnp.where(row8 == r, tiles[r], out)
        return out

    def products(pair, other):
        total = jnp.zeros((CASES, LANES), F32)
        for s in range(2):
            product = pair[s] * other[s]
            for t in range(4):
                total = total + product[:, t * LANES : (t + 1) * LANES]
        return jnp.sum(total, axis=1, keepdims=True)

    def as_row(column, place):
        kept = jnp.where(lane16 == row16 + 16 * place, column, 0.0)
        return jnp.sum(kept, axis=0, keepdims=True)

    def as_column(row, place):
        spread = jnp.broadcast_to(row, (CASES, LANES))
        kept = jnp.where(lane16 == row16 + 16 * place, spread, 0.0)
        return jnp.sum(kept, axis=1, keepdims=True)

    def times(parts, v, s):
        top, rest = split(v)
        both = jnp.concatenate([top, rest], axis=0)
        product = dot(jnp.concatenate([both, both], axis=1), parts[s])
        return product[0:CASES] + product[CASES : 2 * CASES]

    def cut(source, parts):
        for s in range(2):

            @pl.loop(0, 8)
            def _(i):
                at = pl.multiple_of(i * 64, 64)
                top, rest = split(source[s, pl.ds(at, 64)])
                parts[s, pl.ds(at, 64)] = top
                parts[s, pl.ds(at + DOFS, 64)] = rest

    def halo_copies(n):
        make = functools.partial(pltpu.make_async_remote_copy, device_id_type=MESH)
        return (
            make(src_ref=field.at[n, 1], dst_ref=halo.at[n, 0], send_sem=halo_send.at[n, 0],
                 recv_sem=halo_recv.at[n, 0], device_id=(right,)),
            make(src_ref=field.at[n, 0], dst_ref=halo.at[n, 1], send_sem=halo_send.at[n, 1],
                 recv_sem=halo_recv.at[n, 1], device_id=(left,)),
        )

    def send_halo(n, pair):
        field[n, 0] = pair[0]
        field[n, 1] = pair[1]
        for copy in halo_copies(n):
            copy.start()

    def extended(n):
        for copy in halo_copies(n):
            copy.wait()
        return [halo[n, 0], field[n, 0], field[n, 1], halo[n, 1]]

    def to_all(buf, rows, n):
        part = pl.ds(0, rows)
        for o in CHIPS[:-1]:
            pltpu.make_async_remote_copy(
                src_ref=buf.at[0, part], dst_ref=buf.at[place_of(o), part],
                send_sem=all_send.at[n], recv_sem=all_recv.at[n],
                device_id=device(o, 0), device_id_type=MESH,
            ).start()

    def forward(buf, rows, n, first=0, count=64):
        return pltpu.make_async_remote_copy(
            src_ref=buf.at[pl.ds(first, count), pl.ds(0, rows)],
            dst_ref=buf.at[pl.ds(64 + first, count), pl.ds(0, rows)],
            send_sem=fwd_send.at[n], recv_sem=fwd_recv.at[n],
            device_id=device((0, 0, 0), 1), device_id_type=MESH,
        )

    def from_all(buf, rows, n):
        others = buf.at[pl.ds(0, 63), pl.ds(0, rows)]
        await_bytes(others, all_recv.at[n])
        copy = forward(buf, rows, n)
        copy.start()
        await_bytes(others, all_send.at[n])
        copy.wait()

    thirds = (coarse_a, coarse_b, buf1)

    def send_stage(third, stage):
        buf, axis, size = thirds[third], ROUTES[third][stage], 4**stage
        for k in (2, 1, 3):
            pltpu.make_async_remote_copy(
                src_ref=buf.at[pl.ds(0, size)], dst_ref=buf.at[pl.ds(k * size, size)],
                send_sem=stage_send.at[third, stage], recv_sem=stage_recv.at[third, stage],
                device_id=device(steps(axis, k), 0), device_id_type=MESH,
            ).start()

    def await_stage(sems, third, stage):
        await_bytes(thirds[third].at[pl.ds(0, 3 * 4**stage)], sems.at[third, stage])

    load = [load_v[:, s, :] for s in range(2)]
    buf1[0] = jnp.where(row8 == 6, ids, corner_rows(load))

    pl.semaphore_wait(barrier, len(partners))
    for third in range(3):
        send_stage(third, 0)
    def beside(copies):
        made = []
        for i, dev in enumerate((right, left)):
            for src, dst, n in copies(i):
                made.append(
                    pltpu.make_async_remote_copy(
                        src_ref=src, dst_ref=dst, send_sem=side_send.at[n, i],
                        recv_sem=side_recv.at[n, i], device_id=(dev,), device_id_type=MESH,
                    )
                )
        return made

    side_copies = beside(
        lambda i: (
            (map_v, map_side.at[i], 0),
            (buf1.at[0, pl.ds(6, 1)], id_side.at[i], 1),
            (partner_v, partner_side.at[i], 2),
        )
    )
    def upper(block):
        return pl.ds(block * LANES, LANES), pl.ds(block * LANES, DOFS - block * LANES)

    schur_copies = [
        beside(lambda i: ((schur_v.at[1 - i, *upper(b)], schur_side.at[i, *upper(b)], 4 + b),))
        for b in range(4)
    ]
    wide_copies = beside(lambda i: ((field.at[2], halo_wide.at[i], 3),))
    for copy in side_copies:
        copy.start()
    copies[5].wait()
    cut(inverse_v, inverse_parts)
    for third in range(3):
        await_stage(stage_recv, third, 0)
        send_stage(third, 1)
    send_halo(0, [times(inverse_parts, load[s], s) for s in range(2)])
    for third in range(3):
        await_stage(stage_recv, third, 1)
        send_stage(third, 2)
        forward(thirds[third], 8, 2 * third, 0, 16).start()
    copies[6].wait()
    cut(schur_v, schur_parts)
    for copy in side_copies:
        copy.wait()
    for first, i, side in ((0, 0, 1), (96, 1, 0), (128, 0, 0), (160, 1, 1)):
        high, low = split(jnp.concatenate([map_side[i, side], gap], axis=0))
        map_high[first : first + 32] = high
        map_low[first : first + 32] = low
    row48 = iota((48, LANES), 0)
    lane48 = iota((48, LANES), 1)

    def id_column(row):
        kept = jnp.where(row48 == lane48, jnp.broadcast_to(row, (48, LANES)), 0.0)
        return jnp.sum(kept, axis=1, keepdims=True)

    before, after = id_column(id_side[0]), id_column(id_side[1])
    corner = jnp.concatenate(
        [before[24:48], id_column(ids), after[0:24], before[0:24], after[24:48]], axis=0
    ).astype(I32)
    owner = corner // OWN
    inner = corner - owner * OWN
    third_of = inner // 8
    wanted = jnp.concatenate(
        [inner % 8 + jnp.where(third_of == 2, 8, 0), 8 + inner % 8], axis=0
    )
    slots = iota((1, LANES), 1)

    def owned(third):
        digits = [slots // 4**k % 4 for k in range(3)]
        dz, dx, dy = (digits[ROUTES[third].index(axis)] for axis in range(3))
        held = (z - dz) % 4 * 32 + (x - dx) % 4 * 8 + (y - dy) % 4 * 2 + (core + slots // 64) % 2
        one = jnp.where(held == owner, 1.0, 0.0)
        return jnp.concatenate([one, one], axis=0)

    pick = jnp.concatenate(
        [jnp.where(wanted == 8 * t + r, owned(t), 0.0).astype(BF16) for t in range(2) for r in range(8)],
        axis=1,
    )
    for third in range(3):
        await_stage(stage_recv, third, 2)
        forward(thirds[third], 8, 2 * third + 1, 16, 48).start()

    for copy in itertools.chain(*schur_copies[:1]):
        copy.start()

    def await_forward(third):
        forward(thirds[third], 8, 2 * third, 0, 16).wait()
        forward(thirds[third], 8, 2 * third + 1, 16, 48).wait()

    await_forward(0)
    await_forward(1)
    packed = [buf[:, r, :] for buf in (coarse_a, coarse_b) for r in range(8)]
    high, low = split(jnp.concatenate(packed, axis=0))
    found = dot(pick, jnp.concatenate([high, low], axis=1))
    found = found[:, 0:LANES] + found[:, LANES : 2 * LANES]
    at = iota((144, LANES), 1) - 1
    from_a = take_lanes(found[0:144], jnp.clip(at + jnp.where(third_of == 1, 64, 0), 0, LANES - 1))
    from_t = take_lanes(found[144:288], jnp.clip(at + 8 * third_of, 0, LANES - 1))
    window = jnp.where(at < 64, from_a, from_t)
    table[...] = jnp.where((at >= 0) & (at < WIN), window, 0.0)
    bases[...] = jnp.broadcast_to((owner - 1) * OWN - 1, (144, LANES))

    def build(out_ref, first, count):
        @pl.loop(0, 8)
        def _(e):
            everyone = [id_rows[pl.ds(8 * r + e, 1), :] for r in range(6)]
            for k in range(0, count, 16):
                rows = table[first + k : first + k + 16]
                base = bases[first + k : first + k + 16]
                out = pl.ds(pl.multiple_of(e * count + k, 16), 16)
                for r in range(6):
                    place = jnp.broadcast_to(everyone[r], (16, LANES)) - base
                    top, rest = split(take_lanes(rows, jnp.clip(place, 0, LANES - 1)))
                    out_ref[out, r * LANES : (r + 1) * LANES] = top
                    out_ref[out, (r + 6) * LANES : (r + 7) * LANES] = rest

    await_forward(2)
    id_rows[...] = jnp.transpose(buf1[:, 6, :])[0:48].astype(I32)
    build(operator, 0, 96)
    for third in range(3):
        for stage in range(3):
            await_stage(stage_send, third, stage)

    def gathered(buf):
        top, rest = split(jnp.concatenate([buf[:, r, :] for r in range(6)], axis=0))
        both = jnp.concatenate([top, rest], axis=1)
        return jnp.concatenate([both, both], axis=0)

    def spread(everyone, rows_ref, subs, first):
        count = 24 * subs
        product = dot(rows_ref[...], everyone)
        solved = jnp.zeros((count, 2 * LANES), F32)
        lanes = iota((count, 2 * LANES), 1) % LANES // 16
        for e in range(8):
            solved = jnp.where(lanes == e, product[count * e : count * e + count], solved)
        solved = solved[:, 0:LANES] + solved[:, LANES : 2 * LANES]
        padded = []
        for j in range(4):
            if j < subs:
                padded += [solved[24 * j : 24 * j + 24], jnp.zeros((8, LANES), F32)]
            else:
                padded += [jnp.zeros((32, LANES), F32)]
        turned = jnp.transpose(jnp.concatenate(padded, axis=0))
        by_case = turned[0:CASES]
        for e in range(1, 8):
            by_case = by_case + turned[CASES * e : CASES * e + CASES]
        stack = []
        for j in range(subs):
            stack += list(split(jnp.where(lane16 // 32 == j, by_case, 0.0)))
        stack = jnp.concatenate(stack, axis=0)
        maps = slice(first, first + LANES)
        product = dot(stack, map_high[maps]) + dot(stack, map_low[maps])
        return [product[32 * j : 32 * j + 16] + product[32 * j + 16 : 32 * j + 32] for j in range(subs)]

    def around(buf):
        return spread(gathered(buf), operator, 4, 0)

    def add(first, second):
        return [a + b for a, b in zip(first, second)]

    r0 = jumped(add(around(buf1), extended(0)))
    send_halo(1, [times(schur_parts, r0[s], s) for s in range(2)])
    for copy in itertools.chain(*schur_copies[1:]):
        copy.start()
    a = [0.5 * v for v in jumped(extended(1))]

    buf2[0] = corner_rows(a)
    to_all(buf2, 6, 6)
    field[2, 0] = times(inverse_parts, a[0], 0)
    field[2, 1] = times(inverse_parts, a[1], 1)
    for copy in wide_copies:
        copy.start()
    build(operator_wide, 96, 48)
    for copy in itertools.chain(*schur_copies):
        copy.wait()

    @pl.loop(0, 2)
    def _(i):
        for b in range(4):
            for c in range(4):
                first, last = min(b, c) * LANES, max(b, c) * LANES
                block = schur_side[i, first : first + LANES, last : last + LANES]
                top, rest = split(block if b <= c else jnp.transpose(block))
                columns = slice(c * LANES, (c + 1) * LANES)
                side_parts[i, b * LANES : (b + 1) * LANES, columns] = top
                side_parts[i, DOFS + b * LANES : DOFS + (b + 1) * LANES, columns] = rest

    for copy in wide_copies:
        copy.wait()
    from_all(buf2, 6, 6)

    everyone = gathered(buf2)
    near = spread(everyone, operator, 4, 0)
    near = add(near, [halo_wide[0, 1], field[2, 0], field[2, 1], halo_wide[1, 0]])
    far = add(spread(everyone, operator_wide, 2, 128), [halo_wide[0, 0], halo_wide[1, 1]])
    s_a = [far[0], *near, far[1]]
    side_partners = [
        partner_side[0][1:2] - (2 * me - 2) * DOFS, partner_side[1][0:1] - (2 * me + 1) * DOFS
    ]
    partners4 = [side_partners[0], *own_partners, side_partners[1]]
    q4 = [2.0 * jump(s_a[j : j + 3], partners4[j]) for j in range(4)]
    w = [
        0.5 * v
        for v in jumped(
            [
                times(side_parts, q4[0], 0), times(schur_parts, q4[1], 0),
                times(schur_parts, q4[2], 1), times(side_parts, q4[3], 1),
            ]
        )
    ]
    s_a, q = s_a[2:4], q4[1:3]
    dots = as_row(products(r0, a), 0) + as_row(products(a, q), 1)

    buf3[0] = jnp.where(row8 == 6, dots, corner_rows(w))
    to_all(buf3, 7, 7)
    send_halo(4, [times(inverse_parts, w[s], s) for s in range(2)])
    solved_w = extended(4)
    from_all(buf3, 7, 7)

    s_w = add(around(buf3), solved_w)
    total = jnp.sum(buf3[:, 6, :], axis=0, keepdims=True)
    current, curvature = as_column(total, 0), as_column(total, 1)
    step0 = current / curvature
    r1 = [r0[s] - step0 * q[s] for s in range(2)]
    z1 = [a[s] - step0 * w[s] for s in range(2)]
    s_z = [s_a[s] - step0 * s_w[s + 1] for s in range(2)]
    cross = 4.0 * (products(z1, s_a) + products(a, s_z))
    dots = as_row(products(r1, z1), 0) + as_row(4.0 * products(z1, s_z), 1) + as_row(cross, 2)
    buf4[0] = jnp.where(row8 == 0, dots, 0.0)
    for o in CHIPS:
        for c in range(2):
            if place_of(o) + c > 0:
                pltpu.make_async_remote_copy(
                    src_ref=buf4.at[0, pl.ds(0, 1)],
                    dst_ref=buf4.at[place_of(o) + 64 * c, pl.ds(0, 1)],
                    send_sem=all_send.at[8], recv_sem=all_recv.at[8],
                    device_id=device(o, c), device_id_type=MESH,
                ).start()
    u = [2.0 * v for v in jumped(s_w)]
    image = [q[s] - step0 * u[s] for s in range(2)]
    await_bytes(buf4.at[pl.ds(0, 127), pl.ds(0, 1)], all_recv.at[8])
    total = jnp.sum(buf4[:, 0, :], axis=0, keepdims=True)
    following = as_column(total, 0)
    ratio = following / current
    curvature1 = as_column(total, 1) + ratio * as_column(total, 2) + ratio * ratio * curvature
    step1 = following / curvature1
    for s in range(2):
        mult_ref[:, s, :] = step0 * a[s] + step1 * (z1[s] + ratio * a[s])
        resid_ref[:, s, :] = r1[s] - step1 * (image[s] + ratio * q[s])

    await_bytes(buf4.at[pl.ds(0, 127), pl.ds(0, 1)], all_send.at[8])


def per_device(load, schur_inverse, schur, corner_map, corner_ids, coarse_inverse, partner):
    vmem = pltpu.VMEM
    dma = pltpu.SemaphoreType.DMA
    out = jax.ShapeDtypeStruct(load.shape, F32)
    inputs = (load, schur_inverse, schur, corner_map, corner_ids, coarse_inverse, partner)
    parts = vmem((2, 2 * DOFS, DOFS), BF16)
    slots = vmem((128, 8, LANES), F32)
    return pl.pallas_call(
        kernel,
        out_shape=(out, out),
        in_specs=[pl.BlockSpec(memory_space=pltpu.HBM)] * 7,
        out_specs=(pl.BlockSpec(memory_space=vmem),) * 2,
        scratch_shapes=[
            *(vmem(v.shape, v.dtype) for v in inputs),
            parts, parts,
            vmem((256, DOFS), BF16), vmem((256, DOFS), BF16),
            vmem((2, 2, CORNERS, DOFS), F32), vmem((2, 1, LANES), F32),
            vmem((2, 2, DOFS), I32), vmem((2, DOFS, DOFS), F32), parts,
            vmem((144, LANES), F32), vmem((144, LANES), I32), vmem((48, LANES), I32),
            vmem((768, 1536), BF16), vmem((384, 1536), BF16),
            vmem((5, 2, CASES, DOFS), F32), vmem((5, 2, CASES, DOFS), F32),
            vmem((2, 2, CASES, DOFS), F32),
            slots, slots, slots, slots, slots, slots,
            dma((7,)), dma((3, 3)), dma((3, 3)), dma((9,)), dma((9,)), dma((8,)), dma((8,)),
            dma((5, 2)), dma((5, 2)), dma((8, 2)), dma((8, 2)),
        ],
        compiler_params=pltpu.CompilerParams(
            collective_id=0, has_side_effects=True, vmem_limit_bytes=63 << 20
        ),
    )(*inputs)


def solution(mesh):
    in_specs = (
        P(None, "sub", None),
        P("sub", None, None),
        P("sub", None, None),
        P("sub", None, None),
        P("sub", None),
        P("sub", None),
        P("sub", None),
    )
    out_specs = (P(None, "sub", None), P(None, "sub", None))
    return jax.shard_map(
        per_device, mesh=mesh, in_specs=in_specs, out_specs=out_specs, check_vma=False
    )
```

```python
import functools
import itertools

import jax
import jax.numpy as jnp
from jax import lax
from jax.experimental import pallas as pl
from jax.experimental.pallas import tpu as pltpu
from jax.sharding import PartitionSpec as P

MESH = pl.DeviceIdType.MESH
F32, BF16, I32 = jnp.float32, jnp.bfloat16, jnp.int32
CASES, DOFS, CORNERS, OWN, WIN = 16, 512, 24, 24, 72
LANES = 128
HOPS = (0, 1, 2, 1)

CHIPS = sorted(
    itertools.product(range(4), repeat=3), key=lambda o: -sum(HOPS[d] for d in o)
)
ROUTES = ((2, 1, 0), (1, 0, 2), (0, 2, 1))


def place_of(o):
    return sum(o[axis] * 4**k for k, axis in enumerate(ROUTES[2]))


def split(v):
    high = v.astype(BF16)
    return high, (v - high.astype(F32)).astype(BF16)


def await_bytes(ref, sem):
    pltpu.make_async_copy(ref, ref, sem).wait()


def dot(a, b):
    return jnp.dot(a, b, preferred_element_type=F32)


def take_lanes(values, lanes):
    return jnp.take_along_axis(values, lanes, axis=1, mode="promise_in_bounds")


def iota(shape, dim):
    return lax.broadcasted_iota(I32, shape, dim)


def kernel(
    load_hbm, inverse_hbm, schur_hbm, map_hbm, ids_hbm, coarse_hbm, partner_hbm,
    mult_ref, resid_ref,
    load_v, inverse_v, schur_v, map_v, ids_v, coarse_v, partner_v,
    inverse_parts, schur_parts, map_high, map_low, map_side, id_side,
    partner_side, schur_side, side_parts, table, bases, id_rows, operator,
    field, halo, halo_wide, coarse_a, coarse_b, buf1, buf2, buf3, buf4,
    in_sem, stage_send, stage_recv, all_send, all_recv, fwd_send, fwd_recv, halo_send, halo_recv,
    side_send, side_recv,
):
    me = lax.axis_index("sub")
    core, chip = me % 2, me // 2
    y, x, z = chip % 4, chip // 4 % 4, chip // 16
    zs = [(z + i) % 4 * 32 for i in range(4)]
    xs = [(x + i) % 4 * 8 for i in range(4)]
    ys = [(y + i) % 4 * 2 for i in range(4)]
    cs = [core, 1 - core]
    right, left = (me + 1) % 128, (me + 127) % 128

    def device(o, c):
        return (zs[o[0]] + xs[o[1]] + ys[o[2]] + cs[c],)

    def steps(axis, k):
        return tuple(k if i == axis else 0 for i in range(3))

    pairs = (
        (map_hbm, map_v), (load_hbm, load_v), (ids_hbm, ids_v), (coarse_hbm, coarse_v),
        (partner_hbm, partner_v), (inverse_hbm, inverse_v), (schur_hbm, schur_v),
    )
    copies = [pltpu.make_async_copy(a, b, in_sem.at[i]) for i, (a, b) in enumerate(pairs)]
    for copy in copies:
        copy.start()

    barrier = pltpu.get_barrier_semaphore()
    partners = [device(steps(axis, k), 0) for axis in range(3) for k in (2, 1, 3)]
    partners += [(jnp.where(core == 0, left, right),), device((0, 0, 0), 1)]
    for partner in partners:
        pl.semaphore_signal(barrier, inc=1, device_id=partner, device_id_type=MESH)

    lane8 = iota((8, LANES), 1)
    row8 = iota((8, LANES), 0)
    lane16 = iota((CASES, LANES), 1)
    row16 = iota((CASES, LANES), 0)

    for copy in copies[:5]:
        copy.wait()
    gap = jnp.zeros((8, DOFS), F32)
    map_high[192:256] = jnp.zeros((64, DOFS), BF16)
    map_low[192:256] = jnp.zeros((64, DOFS), BF16)
    own_maps = [map_v[s] for s in range(2)]
    for s in range(2):
        high, low = split(jnp.concatenate([own_maps[s], gap], axis=0))
        map_high[32 * s : 32 * s + 32] = high
        map_low[32 * s : 32 * s + 32] = low

    coarse = jnp.concatenate([coarse_v[...], jnp.zeros((OWN, LANES - WIN), F32)], axis=1)
    m0, m1, m2 = coarse[0:8], coarse[8:16], coarse[16:24]
    ids = jnp.concatenate([ids_v[...].astype(F32), jnp.zeros((2, LANES - CORNERS), F32)], axis=1)
    ids = jnp.where(lane8[0:1] < CORNERS, ids[0:1], pltpu.roll(ids, CORNERS, 1)[1:2])
    coarse_a[0] = jnp.where(lane8 < 64, m0, pltpu.roll(m1, 64, 1))
    second = jnp.where(lane8 < 64, m2, m0)
    second = jnp.where(lane8 >= 72, pltpu.roll(m1, 8, 1), second)
    second = jnp.where(lane8 >= 80, pltpu.roll(m2, 16, 1), second)
    coarse_b[0] = jnp.where(lane8 >= 88, 0.0, second)

    def jump(window, partners):
        columns = []
        for t in range(4):
            at = slice(t * LANES, (t + 1) * LANES)
            flat = jnp.broadcast_to(partners[:, at], (CASES, LANES))
            lanes, block = flat % LANES, flat // LANES
            mate = jnp.zeros((CASES, LANES), F32)
            for b in range(12):
                source = window[b // 4][:, b % 4 * LANES : (b % 4 + 1) * LANES]
                mate = jnp.where(block == b, take_lanes(source, lanes), mate)
            columns.append(window[1][:, at] - mate)
        return jnp.concatenate(columns, axis=1)

    own_partners = [partner_v[s : s + 1] - (2 * me + s - 1) * DOFS for s in range(2)]

    def jumped(extended):
        return [jump(extended[s : s + 3], own_partners[s]) for s in range(2)]

    def corner_rows(pair):
        tiles = []
        for s in range(2):
            high, low = split(pair[s])
            both = jnp.concatenate([high] * 8 + [low] * 8, axis=0)
            at = slice(32 * s, 32 * s + 32)
            maps = jnp.concatenate([map_high[at], map_low[at]], axis=0)
            product = lax.dot_general(
                maps, both, (((1,), (1,)), ((), ())), preferred_element_type=F32
            )
            rows = product[0:32] + product[32:64]
            rows = rows[:, 0:LANES] + rows[:, LANES : 2 * LANES]
            for k in range(3):
                kept = jnp.where(lane8 // 16 == row8, rows[8 * k : 8 * k + 8], 0.0)
                tiles.append(jnp.sum(kept, axis=0, keepdims=True))
        out = jnp.zeros((8, LANES), F32)
        for r in range(6):
            out = jnp.where(row8 == r, tiles[r], out)
        return out

    def products(pair, other):
        total = jnp.zeros((CASES, LANES), F32)
        for s in range(2):
            product = pair[s] * other[s]
            for t in range(4):
                total = total + product[:, t * LANES : (t + 1) * LANES]
        return jnp.sum(total, axis=1, keepdims=True)

    def as_row(column, place):
        kept = jnp.where(lane16 == row16 + 16 * place, column, 0.0)
        return jnp.sum(kept, axis=0, keepdims=True)

    def as_column(row, place):
        spread = jnp.broadcast_to(row, (CASES, LANES))
        kept = jnp.where(lane16 == row16 + 16 * place, spread, 0.0)
        return jnp.sum(kept, axis=1, keepdims=True)

    def times(parts, v, s):
        top, rest = split(v)
        both = jnp.concatenate([top, rest], axis=0)
        product = dot(jnp.concatenate([both, both], axis=1), parts[s])
        return product[0:CASES] + product[CASES : 2 * CASES]

    def cut(source, parts):
        for s in range(2):

            @pl.loop(0, 8)
            def _(i):
                at = pl.multiple_of(i * 64, 64)
                top, rest = split(source[s, pl.ds(at, 64)])
                parts[s, pl.ds(at, 64)] = top
                parts[s, pl.ds(at + DOFS, 64)] = rest

    def halo_copies(n):
        make = functools.partial(pltpu.make_async_remote_copy, device_id_type=MESH)
        return (
            make(src_ref=field.at[n, 1], dst_ref=halo.at[n, 0], send_sem=halo_send.at[n, 0],
                 recv_sem=halo_recv.at[n, 0], device_id=(right,)),
            make(src_ref=field.at[n, 0], dst_ref=halo.at[n, 1], send_sem=halo_send.at[n, 1],
                 recv_sem=halo_recv.at[n, 1], device_id=(left,)),
        )

    def send_halo(n, pair):
        field[n, 0] = pair[0]
        field[n, 1] = pair[1]
        for copy in halo_copies(n):
            copy.start()

    def extended(n):
        for copy in halo_copies(n):
            copy.wait()
        return [halo[n, 0], field[n, 0], field[n, 1], halo[n, 1]]

    def to_all(buf, rows, n):
        part = pl.ds(0, rows)
        for o in CHIPS[:-1]:
            pltpu.make_async_remote_copy(
                src_ref=buf.at[0, part], dst_ref=buf.at[place_of(o), part],
                send_sem=all_send.at[n], recv_sem=all_recv.at[n],
                device_id=device(o, 0), device_id_type=MESH,
            ).start()

    def forward(buf, rows, n, first=0, count=64):
        return pltpu.make_async_remote_copy(
            src_ref=buf.at[pl.ds(first, count), pl.ds(0, rows)],
            dst_ref=buf.at[pl.ds(64 + first, count), pl.ds(0, rows)],
            send_sem=fwd_send.at[n], recv_sem=fwd_recv.at[n],
            device_id=device((0, 0, 0), 1), device_id_type=MESH,
        )

    def from_all(buf, rows, n):
        others = buf.at[pl.ds(0, 63), pl.ds(0, rows)]
        await_bytes(others, all_recv.at[n])
        copy = forward(buf, rows, n)
        copy.start()
        await_bytes(others, all_send.at[n])
        copy.wait()

    thirds = (coarse_a, coarse_b, buf1)

    def send_stage(third, stage):
        buf, axis, size = thirds[third], ROUTES[third][stage], 4**stage
        for k in (2, 1, 3):
            pltpu.make_async_remote_copy(
                src_ref=buf.at[pl.ds(0, size)], dst_ref=buf.at[pl.ds(k * size, size)],
                send_sem=stage_send.at[third, stage], recv_sem=stage_recv.at[third, stage],
                device_id=device(steps(axis, k), 0), device_id_type=MESH,
            ).start()

    def await_stage(sems, third, stage):
        await_bytes(thirds[third].at[pl.ds(0, 3 * 4**stage)], sems.at[third, stage])

    load = [load_v[:, s, :] for s in range(2)]
    buf1[0] = jnp.where(row8 == 6, ids, corner_rows(load))

    pl.semaphore_wait(barrier, len(partners))
    for third in range(3):
        send_stage(third, 0)
    def beside(copies):
        made = []
        for i, dev in enumerate((right, left)):
            for src, dst, n in copies(i):
                made.append(
                    pltpu.make_async_remote_copy(
                        src_ref=src, dst_ref=dst, send_sem=side_send.at[n, i],
                        recv_sem=side_recv.at[n, i], device_id=(dev,), device_id_type=MESH,
                    )
                )
        return made

    side_copies = beside(
        lambda i: (
            (map_v, map_side.at[i], 0),
            (buf1.at[0, pl.ds(6, 1)], id_side.at[i], 1),
            (partner_v, partner_side.at[i], 2),
        )
    )
    def upper(block):
        return pl.ds(block * LANES, LANES), pl.ds(block * LANES, DOFS - block * LANES)

    schur_copies = [
        beside(lambda i: ((schur_v.at[1 - i, *upper(b)], schur_side.at[i, *upper(b)], 4 + b),))
        for b in range(4)
    ]
    wide_copies = beside(lambda i: ((field.at[2], halo_wide.at[i], 3),))
    for copy in side_copies:
        copy.start()
    copies[5].wait()
    cut(inverse_v, inverse_parts)
    for third in range(3):
        await_stage(stage_recv, third, 0)
        send_stage(third, 1)
    send_halo(0, [times(inverse_parts, load[s], s) for s in range(2)])
    for third in range(3):
        await_stage(stage_recv, third, 1)
        send_stage(third, 2)
        forward(thirds[third], 8, 2 * third, 0, 16).start()
    copies[6].wait()
    cut(schur_v, schur_parts)
    for copy in side_copies:
        copy.wait()
    for first, i, side in ((64, 0, 1), (96, 1, 0), (128, 0, 0), (160, 1, 1)):
        high, low = split(jnp.concatenate([map_side[i, side], gap], axis=0))
        map_high[first : first + 32] = high
        map_low[first : first + 32] = low
    row48 = iota((48, LANES), 0)
    lane48 = iota((48, LANES), 1)

    def id_column(row):
        kept = jnp.where(row48 == lane48, jnp.broadcast_to(row, (48, LANES)), 0.0)
        return jnp.sum(kept, axis=1, keepdims=True)

    before, after = id_column(id_side[0]), id_column(id_side[1])
    corner = jnp.concatenate(
        [id_column(ids), before[24:48], after[0:24], before[0:24], after[24:48]], axis=0
    ).astype(I32)
    owner = corner // OWN
    inner = corner - owner * OWN
    third_of = inner // 8
    wanted = jnp.concatenate(
        [inner % 8 + jnp.where(third_of == 2, 8, 0), 8 + inner % 8], axis=0
    )
    slots = iota((1, LANES), 1)

    def owned(third):
        digits = [slots // 4**k % 4 for k in range(3)]
        dz, dx, dy = (digits[ROUTES[third].index(axis)] for axis in range(3))
        held = (z - dz) % 4 * 32 + (x - dx) % 4 * 8 + (y - dy) % 4 * 2 + (core + slots // 64) % 2
        one = jnp.where(held == owner, 1.0, 0.0)
        return jnp.concatenate([one, one], axis=0)

    pick = jnp.concatenate(
        [jnp.where(wanted == 8 * t + r, owned(t), 0.0).astype(BF16) for t in range(2) for r in range(8)],
        axis=1,
    )
    for third in range(3):
        await_stage(stage_recv, third, 2)
        forward(thirds[third], 8, 2 * third + 1, 16, 48).start()

    for copy in itertools.chain(*schur_copies[:1]):
        copy.start()

    def await_forward(third):
        forward(thirds[third], 8, 2 * third, 0, 16).wait()
        forward(thirds[third], 8, 2 * third + 1, 16, 48).wait()

    await_forward(0)
    await_forward(1)
    packed = [buf[:, r, :] for buf in (coarse_a, coarse_b) for r in range(8)]
    high, low = split(jnp.concatenate(packed, axis=0))
    found = dot(pick, jnp.concatenate([high, low], axis=1))
    found = found[:, 0:LANES] + found[:, LANES : 2 * LANES]
    at = iota((144, LANES), 1) - 1
    from_a = take_lanes(found[0:144], jnp.clip(at + jnp.where(third_of == 1, 64, 0), 0, LANES - 1))
    from_t = take_lanes(found[144:288], jnp.clip(at + 8 * third_of, 0, LANES - 1))
    window = jnp.where(at < 64, from_a, from_t)
    table[...] = jnp.where((at >= 0) & (at < WIN), window, 0.0)
    bases[...] = jnp.broadcast_to((owner - 1) * OWN - 1, (144, LANES))

    def build(first, count):
        @pl.loop(0, 8)
        def _(e):
            everyone = [id_rows[pl.ds(8 * r + e, 1), :] for r in range(6)]
            for k in range(first, first + count, 16):
                rows = table[k : k + 16]
                base = bases[k : k + 16]
                out = pl.ds(pl.multiple_of(k // 48 * 384 + e * 48 + k % 48, 16), 16)
                for r in range(6):
                    place = jnp.broadcast_to(everyone[r], (16, LANES)) - base
                    top, rest = split(take_lanes(rows, jnp.clip(place, 0, LANES - 1)))
                    operator[out, r * LANES : (r + 1) * LANES] = top
                    operator[out, (r + 6) * LANES : (r + 7) * LANES] = rest

    await_forward(2)
    id_rows[...] = jnp.transpose(buf1[:, 6, :])[0:48].astype(I32)
    build(0, 96)
    for third in range(3):
        for stage in range(3):
            await_stage(stage_send, third, stage)

    def gathered(buf):
        top, rest = split(jnp.concatenate([buf[:, r, :] for r in range(6)], axis=0))
        both = jnp.concatenate([top, rest], axis=1)
        return jnp.concatenate([both, both], axis=0)

    def spread(everyone, first, count):
        padded = []
        lanes = iota((48, 2 * LANES), 1) % LANES // 16
        for pair in range(first, first + count):
            solved = jnp.zeros((48, 2 * LANES), F32)
            for half in range(2):
                at = 384 * pair + 192 * half
                product = dot(operator[at : at + 192], everyone)
                for e in range(4):
                    solved = jnp.where(lanes == 4 * half + e, product[48 * e : 48 * e + 48], solved)
            solved = solved[:, 0:LANES] + solved[:, LANES : 2 * LANES]
            zero = jnp.zeros((8, LANES), F32)
            padded += [solved[0:24], zero, solved[24:48], zero]
        if count == 1:
            padded.append(jnp.zeros((64, LANES), F32))
        turned = jnp.transpose(jnp.concatenate(padded, axis=0))
        by_case = turned[0:CASES]
        for e in range(1, 8):
            by_case = by_case + turned[CASES * e : CASES * e + CASES]
        stack = []
        for j in range(2 * count):
            stack += list(split(jnp.where(lane16 // 32 == j, by_case, 0.0)))
        stack = jnp.concatenate(stack, axis=0)
        maps = slice(64 * first, 64 * first + LANES)
        product = dot(stack, map_high[maps]) + dot(stack, map_low[maps])
        return [
            product[32 * j : 32 * j + 16] + product[32 * j + 16 : 32 * j + 32]
            for j in range(2 * count)
        ]

    def around(everyone):
        own0, own1, before, after = spread(everyone, 0, 2)
        return [before, own0, own1, after]

    def add(first, second):
        return [a + b for a, b in zip(first, second)]

    r0 = jumped(add(around(gathered(buf1)), extended(0)))
    send_halo(1, [times(schur_parts, r0[s], s) for s in range(2)])
    for copy in itertools.chain(*schur_copies[1:]):
        copy.start()
    a = [0.5 * v for v in jumped(extended(1))]

    buf2[0] = corner_rows(a)
    to_all(buf2, 6, 6)
    field[2, 0] = times(inverse_parts, a[0], 0)
    field[2, 1] = times(inverse_parts, a[1], 1)
    for copy in wide_copies:
        copy.start()
    build(96, 48)
    for copy in itertools.chain(*schur_copies):
        copy.wait()

    @pl.loop(0, 2)
    def _(i):
        for b in range(4):
            for c in range(4):
                first, last = min(b, c) * LANES, max(b, c) * LANES
                block = schur_side[i, first : first + LANES, last : last + LANES]
                top, rest = split(block if b <= c else jnp.transpose(block))
                columns = slice(c * LANES, (c + 1) * LANES)
                side_parts[i, b * LANES : (b + 1) * LANES, columns] = top
                side_parts[i, DOFS + b * LANES : DOFS + (b + 1) * LANES, columns] = rest

    for copy in wide_copies:
        copy.wait()
    from_all(buf2, 6, 6)

    everyone = gathered(buf2)
    near = around(everyone)
    near = add(near, [halo_wide[0, 1], field[2, 0], field[2, 1], halo_wide[1, 0]])
    far = add(spread(everyone, 2, 1), [halo_wide[0, 0], halo_wide[1, 1]])
    s_a = [far[0], *near, far[1]]
    side_partners = [
        partner_side[0][1:2] - (2 * me - 2) * DOFS, partner_side[1][0:1] - (2 * me + 1) * DOFS
    ]
    partners4 = [side_partners[0], *own_partners, side_partners[1]]
    q4 = [2.0 * jump(s_a[j : j + 3], partners4[j]) for j in range(4)]
    w = [
        0.5 * v
        for v in jumped(
            [
                times(side_parts, q4[0], 0), times(schur_parts, q4[1], 0),
                times(schur_parts, q4[2], 1), times(side_parts, q4[3], 1),
            ]
        )
    ]
    s_a, q = s_a[2:4], q4[1:3]
    dots = as_row(products(r0, a), 0) + as_row(products(a, q), 1)

    buf3[0] = jnp.where(row8 == 6, dots, corner_rows(w))
    to_all(buf3, 7, 7)
    send_halo(4, [times(inverse_parts, w[s], s) for s in range(2)])
    solved_w = extended(4)
    from_all(buf3, 7, 7)

    everyone = gathered(buf3)
    s_w = add(spread(everyone, 0, 1), solved_w[1:3])
    total = jnp.sum(buf3[:, 6, :], axis=0, keepdims=True)
    current, curvature = as_column(total, 0), as_column(total, 1)
    step0 = current / curvature
    r1 = [r0[s] - step0 * q[s] for s in range(2)]
    z1 = [a[s] - step0 * w[s] for s in range(2)]
    s_z = [s_a[s] - step0 * s_w[s] for s in range(2)]
    cross = 4.0 * (products(z1, s_a) + products(a, s_z))
    dots = as_row(products(r1, z1), 0) + as_row(4.0 * products(z1, s_z), 1) + as_row(cross, 2)
    buf4[0] = jnp.where(row8 == 0, dots, 0.0)
    for o in CHIPS:
        for c in range(2):
            if place_of(o) + c > 0:
                pltpu.make_async_remote_copy(
                    src_ref=buf4.at[0, pl.ds(0, 1)],
                    dst_ref=buf4.at[place_of(o) + 64 * c, pl.ds(0, 1)],
                    send_sem=all_send.at[8], recv_sem=all_recv.at[8],
                    device_id=device(o, c), device_id_type=MESH,
                ).start()
    before, after = add(spread(everyone, 1, 1), [solved_w[0], solved_w[3]])
    u = [2.0 * v for v in jumped([before, *s_w, after])]
    image = [q[s] - step0 * u[s] for s in range(2)]
    await_bytes(buf4.at[pl.ds(0, 127), pl.ds(0, 1)], all_recv.at[8])
    total = jnp.sum(buf4[:, 0, :], axis=0, keepdims=True)
    following = as_column(total, 0)
    ratio = following / current
    curvature1 = as_column(total, 1) + ratio * as_column(total, 2) + ratio * ratio * curvature
    step1 = following / curvature1
    for s in range(2):
        mult_ref[:, s, :] = step0 * a[s] + step1 * (z1[s] + ratio * a[s])
        resid_ref[:, s, :] = r1[s] - step1 * (image[s] + ratio * q[s])

    await_bytes(buf4.at[pl.ds(0, 127), pl.ds(0, 1)], all_send.at[8])


def per_device(load, schur_inverse, schur, corner_map, corner_ids, coarse_inverse, partner):
    vmem = pltpu.VMEM
    dma = pltpu.SemaphoreType.DMA
    out = jax.ShapeDtypeStruct(load.shape, F32)
    inputs = (load, schur_inverse, schur, corner_map, corner_ids, coarse_inverse, partner)
    parts = vmem((2, 2 * DOFS, DOFS), BF16)
    slots = vmem((128, 8, LANES), F32)
    return pl.pallas_call(
        kernel,
        out_shape=(out, out),
        in_specs=[pl.BlockSpec(memory_space=pltpu.HBM)] * 7,
        out_specs=(pl.BlockSpec(memory_space=vmem),) * 2,
        scratch_shapes=[
            *(vmem(v.shape, v.dtype) for v in inputs),
            parts, parts,
            vmem((256, DOFS), BF16), vmem((256, DOFS), BF16),
            vmem((2, 2, CORNERS, DOFS), F32), vmem((2, 1, LANES), F32),
            vmem((2, 2, DOFS), I32), vmem((2, DOFS, DOFS), F32), parts,
            vmem((144, LANES), F32), vmem((144, LANES), I32), vmem((48, LANES), I32),
            vmem((1152, 1536), BF16),
            vmem((5, 2, CASES, DOFS), F32), vmem((5, 2, CASES, DOFS), F32),
            vmem((2, 2, CASES, DOFS), F32),
            slots, slots, slots, slots, slots, slots,
            dma((7,)), dma((3, 3)), dma((3, 3)), dma((9,)), dma((9,)), dma((8,)), dma((8,)),
            dma((5, 2)), dma((5, 2)), dma((8, 2)), dma((8, 2)),
        ],
        compiler_params=pltpu.CompilerParams(
            collective_id=0, has_side_effects=True, vmem_limit_bytes=63 << 20
        ),
    )(*inputs)


def solution(mesh):
    in_specs = (
        P(None, "sub", None),
        P("sub", None, None),
        P("sub", None, None),
        P("sub", None, None),
        P("sub", None),
        P("sub", None),
        P("sub", None),
    )
    out_specs = (P(None, "sub", None), P(None, "sub", None))
    return jax.shard_map(
        per_device, mesh=mesh, in_specs=in_specs, out_specs=out_specs, check_vma=False
    )
```

```python
import functools
import itertools

import jax
import jax.numpy as jnp
from jax import lax
from jax.experimental import pallas as pl
from jax.experimental.pallas import tpu as pltpu
from jax.sharding import PartitionSpec as P

MESH = pl.DeviceIdType.MESH
F32, BF16, I32 = jnp.float32, jnp.bfloat16, jnp.int32
CASES, DOFS, CORNERS, OWN, WIN = 16, 512, 24, 24, 72
LANES = 128
HOPS = (0, 1, 2, 1)

CHIPS = sorted(
    itertools.product(range(4), repeat=3), key=lambda o: -sum(HOPS[d] for d in o)
)
ROUTES = ((2, 1, 0), (1, 0, 2), (0, 2, 1))


def place_of(o):
    return sum(o[axis] * 4**k for k, axis in enumerate(ROUTES[2]))


def split(v):
    high = v.astype(BF16)
    return high, (v - high.astype(F32)).astype(BF16)


def await_bytes(ref, sem):
    pltpu.make_async_copy(ref, ref, sem).wait()


def dot(a, b):
    return jnp.dot(a, b, preferred_element_type=F32)


def take_lanes(values, lanes):
    return jnp.take_along_axis(values, lanes, axis=1, mode="promise_in_bounds")


def iota(shape, dim):
    return lax.broadcasted_iota(I32, shape, dim)


def kernel(
    load_hbm, inverse_hbm, schur_hbm, map_hbm, ids_hbm, coarse_hbm, partner_hbm,
    mult_ref, resid_ref,
    load_v, inverse_v, schur_v, map_v, ids_v, coarse_v, partner_v,
    inverse_parts, schur_parts, map_high, map_low, map_side, id_side,
    partner_side, schur_side, side_parts, table, bases, id_rows, operator,
    field, halo, halo_wide, coarse_a, coarse_b, buf1, buf2, buf3, buf4,
    in_sem, stage_send, stage_recv, all_send, all_recv, fwd_send, fwd_recv, halo_send, halo_recv,
    side_send, side_recv,
):
    me = lax.axis_index("sub")
    core, chip = me % 2, me // 2
    y, x, z = chip % 4, chip // 4 % 4, chip // 16
    zs = [(z + i) % 4 * 32 for i in range(4)]
    xs = [(x + i) % 4 * 8 for i in range(4)]
    ys = [(y + i) % 4 * 2 for i in range(4)]
    cs = [core, 1 - core]
    right, left = (me + 1) % 128, (me + 127) % 128

    def device(o, c):
        return (zs[o[0]] + xs[o[1]] + ys[o[2]] + cs[c],)

    def steps(axis, k):
        return tuple(k if i == axis else 0 for i in range(3))

    pairs = (
        (map_hbm, map_v), (load_hbm, load_v), (ids_hbm, ids_v), (coarse_hbm, coarse_v),
        (partner_hbm, partner_v), (inverse_hbm, inverse_v), (schur_hbm, schur_v),
    )
    copies = [pltpu.make_async_copy(a, b, in_sem.at[i]) for i, (a, b) in enumerate(pairs)]
    for copy in copies:
        copy.start()

    barrier = pltpu.get_barrier_semaphore()
    partners = [device(steps(axis, k), 0) for axis in range(3) for k in (2, 1, 3)]
    partners += [(jnp.where(core == 0, left, right),), device((0, 0, 0), 1)]
    for partner in partners:
        pl.semaphore_signal(barrier, inc=1, device_id=partner, device_id_type=MESH)

    lane8 = iota((8, LANES), 1)
    row8 = iota((8, LANES), 0)
    lane16 = iota((CASES, LANES), 1)
    row16 = iota((CASES, LANES), 0)

    for copy in copies[:5]:
        copy.wait()
    gap = jnp.zeros((8, DOFS), F32)
    map_high[192:256] = jnp.zeros((64, DOFS), BF16)
    map_low[192:256] = jnp.zeros((64, DOFS), BF16)
    own_maps = [map_v[s] for s in range(2)]
    for s in range(2):
        high, low = split(jnp.concatenate([own_maps[s], gap], axis=0))
        map_high[32 * s : 32 * s + 32] = high
        map_low[32 * s : 32 * s + 32] = low

    coarse = jnp.concatenate([coarse_v[...], jnp.zeros((OWN, LANES - WIN), F32)], axis=1)
    m0, m1, m2 = coarse[0:8], coarse[8:16], coarse[16:24]
    ids = jnp.concatenate([ids_v[...].astype(F32), jnp.zeros((2, LANES - CORNERS), F32)], axis=1)
    ids = jnp.where(lane8[0:1] < CORNERS, ids[0:1], pltpu.roll(ids, CORNERS, 1)[1:2])
    coarse_a[0] = jnp.where(lane8 < 64, m0, pltpu.roll(m1, 64, 1))
    second = jnp.where(lane8 < 64, m2, m0)
    second = jnp.where(lane8 >= 72, pltpu.roll(m1, 8, 1), second)
    second = jnp.where(lane8 >= 80, pltpu.roll(m2, 16, 1), second)
    coarse_b[0] = jnp.where(lane8 >= 88, 0.0, second)

    def jump(window, partners):
        columns = []
        for t in range(4):
            at = slice(t * LANES, (t + 1) * LANES)
            flat = jnp.broadcast_to(partners[:, at], (CASES, LANES))
            lanes, block = flat % LANES, flat // LANES
            mate = jnp.zeros((CASES, LANES), F32)
            for b in range(12):
                source = window[b // 4][:, b % 4 * LANES : (b % 4 + 1) * LANES]
                mate = jnp.where(block == b, take_lanes(source, lanes), mate)
            columns.append(window[1][:, at] - mate)
        return jnp.concatenate(columns, axis=1)

    own_partners = [partner_v[s : s + 1] - (2 * me + s - 1) * DOFS for s in range(2)]

    def jumped(extended):
        return [jump(extended[s : s + 3], own_partners[s]) for s in range(2)]

    def corner_rows(pair):
        tiles = []
        for s in range(2):
            high, low = split(pair[s])
            both = jnp.concatenate([high] * 8 + [low] * 8, axis=0)
            at = slice(32 * s, 32 * s + 32)
            maps = jnp.concatenate([map_high[at], map_low[at]], axis=0)
            product = lax.dot_general(
                maps, both, (((1,), (1,)), ((), ())), preferred_element_type=F32
            )
            rows = product[0:32] + product[32:64]
            rows = rows[:, 0:LANES] + rows[:, LANES : 2 * LANES]
            for k in range(3):
                kept = jnp.where(lane8 // 16 == row8, rows[8 * k : 8 * k + 8], 0.0)
                tiles.append(jnp.sum(kept, axis=0, keepdims=True))
        out = jnp.zeros((8, LANES), F32)
        for r in range(6):
            out = jnp.where(row8 == r, tiles[r], out)
        return out

    def products(pair, other):
        total = jnp.zeros((CASES, LANES), F32)
        for s in range(2):
            product = pair[s] * other[s]
            for t in range(4):
                total = total + product[:, t * LANES : (t + 1) * LANES]
        return jnp.sum(total, axis=1, keepdims=True)

    def as_row(column, place):
        kept = jnp.where(lane16 == row16 + 16 * place, column, 0.0)
        return jnp.sum(kept, axis=0, keepdims=True)

    def as_column(row, place):
        spread = jnp.broadcast_to(row, (CASES, LANES))
        kept = jnp.where(lane16 == row16 + 16 * place, spread, 0.0)
        return jnp.sum(kept, axis=1, keepdims=True)

    def times(parts, v, s):
        top, rest = split(v)
        both = jnp.concatenate([top, rest], axis=0)
        product = dot(jnp.concatenate([both, both], axis=1), parts[s])
        return product[0:CASES] + product[CASES : 2 * CASES]

    def cut(source, parts):
        for s in range(2):

            @pl.loop(0, 8)
            def _(i):
                at = pl.multiple_of(i * 64, 64)
                top, rest = split(source[s, pl.ds(at, 64)])
                parts[s, pl.ds(at, 64)] = top
                parts[s, pl.ds(at + DOFS, 64)] = rest

    def halo_copies(n):
        make = functools.partial(pltpu.make_async_remote_copy, device_id_type=MESH)
        return (
            make(src_ref=field.at[n, 1], dst_ref=halo.at[n, 0], send_sem=halo_send.at[n, 0],
                 recv_sem=halo_recv.at[n, 0], device_id=(right,)),
            make(src_ref=field.at[n, 0], dst_ref=halo.at[n, 1], send_sem=halo_send.at[n, 1],
                 recv_sem=halo_recv.at[n, 1], device_id=(left,)),
        )

    def send_halo(n, pair):
        field[n, 0] = pair[0]
        field[n, 1] = pair[1]
        for copy in halo_copies(n):
            copy.start()

    def extended(n):
        for copy in halo_copies(n):
            copy.wait()
        return [halo[n, 0], field[n, 0], field[n, 1], halo[n, 1]]

    def to_all(buf, rows, n):
        part = pl.ds(0, rows)
        for o in CHIPS[:-1]:
            pltpu.make_async_remote_copy(
                src_ref=buf.at[0, part], dst_ref=buf.at[place_of(o), part],
                send_sem=all_send.at[n], recv_sem=all_recv.at[n],
                device_id=device(o, 0), device_id_type=MESH,
            ).start()

    def forward(buf, rows, n, first=0, count=64):
        return pltpu.make_async_remote_copy(
            src_ref=buf.at[pl.ds(first, count), pl.ds(0, rows)],
            dst_ref=buf.at[pl.ds(64 + first, count), pl.ds(0, rows)],
            send_sem=fwd_send.at[n], recv_sem=fwd_recv.at[n],
            device_id=device((0, 0, 0), 1), device_id_type=MESH,
        )

    def from_all(buf, rows, n):
        others = buf.at[pl.ds(0, 63), pl.ds(0, rows)]
        await_bytes(others, all_recv.at[n])
        copy = forward(buf, rows, n)
        copy.start()
        await_bytes(others, all_send.at[n])
        copy.wait()

    thirds = (coarse_a, coarse_b, buf1)

    def send_stage(third, stage):
        buf, axis, size = thirds[third], ROUTES[third][stage], 4**stage
        for k in (2, 1, 3):
            pltpu.make_async_remote_copy(
                src_ref=buf.at[pl.ds(0, size)], dst_ref=buf.at[pl.ds(k * size, size)],
                send_sem=stage_send.at[third, stage], recv_sem=stage_recv.at[third, stage],
                device_id=device(steps(axis, k), 0), device_id_type=MESH,
            ).start()

    def await_stage(sems, third, stage):
        await_bytes(thirds[third].at[pl.ds(0, 3 * 4**stage)], sems.at[third, stage])

    load = [load_v[:, s, :] for s in range(2)]
    buf1[0] = jnp.where(row8 == 6, ids, corner_rows(load))

    pl.semaphore_wait(barrier, len(partners))
    for third in range(3):
        send_stage(third, 0)
    def beside(copies):
        made = []
        for i, dev in enumerate((right, left)):
            for src, dst, n in copies(i):
                made.append(
                    pltpu.make_async_remote_copy(
                        src_ref=src, dst_ref=dst, send_sem=side_send.at[n, i],
                        recv_sem=side_recv.at[n, i], device_id=(dev,), device_id_type=MESH,
                    )
                )
        return made

    side_copies = beside(
        lambda i: (
            (map_v, map_side.at[i], 0),
            (buf1.at[0, pl.ds(6, 1)], id_side.at[i], 1),
            (partner_v, partner_side.at[i], 2),
        )
    )
    def upper(block):
        return pl.ds(block * LANES, LANES), pl.ds(block * LANES, DOFS - block * LANES)

    schur_copies = [
        beside(lambda i: ((schur_v.at[1 - i, *upper(b)], schur_side.at[i, *upper(b)], 4 + b),))
        for b in range(4)
    ]
    wide_copies = beside(lambda i: ((field.at[2], halo_wide.at[i], 3),))
    for copy in side_copies:
        copy.start()
    copies[5].wait()
    cut(inverse_v, inverse_parts)
    for third in range(3):
        await_stage(stage_recv, third, 0)
        send_stage(third, 1)
    send_halo(0, [times(inverse_parts, load[s], s) for s in range(2)])
    for third in range(3):
        await_stage(stage_recv, third, 1)
        send_stage(third, 2)
        forward(thirds[third], 8, 2 * third, 0, 16).start()
    copies[6].wait()
    cut(schur_v, schur_parts)
    for copy in side_copies:
        copy.wait()
    for first, i, side in ((64, 0, 1), (96, 1, 0), (128, 0, 0), (160, 1, 1)):
        high, low = split(jnp.concatenate([map_side[i, side], gap], axis=0))
        map_high[first : first + 32] = high
        map_low[first : first + 32] = low
    row48 = iota((48, LANES), 0)
    lane48 = iota((48, LANES), 1)

    def id_column(row):
        kept = jnp.where(row48 == lane48, jnp.broadcast_to(row, (48, LANES)), 0.0)
        return jnp.sum(kept, axis=1, keepdims=True)

    before, after = id_column(id_side[0]), id_column(id_side[1])
    corner = jnp.concatenate(
        [id_column(ids), before[24:48], after[0:24], before[0:24], after[24:48]], axis=0
    ).astype(I32)
    owner = corner // OWN
    inner = corner - owner * OWN
    third_of = inner // 8
    wanted = jnp.concatenate(
        [inner % 8 + jnp.where(third_of == 2, 8, 0), 8 + inner % 8], axis=0
    )
    slots = iota((1, LANES), 1)

    def owned(third):
        digits = [slots // 4**k % 4 for k in range(3)]
        dz, dx, dy = (digits[ROUTES[third].index(axis)] for axis in range(3))
        held = (z - dz) % 4 * 32 + (x - dx) % 4 * 8 + (y - dy) % 4 * 2 + (core + slots // 64) % 2
        one = jnp.where(held == owner, 1.0, 0.0)
        return jnp.concatenate([one, one], axis=0)

    pick = jnp.concatenate(
        [jnp.where(wanted == 8 * t + r, owned(t), 0.0).astype(BF16) for t in range(2) for r in range(8)],
        axis=1,
    )
    for third in range(3):
        await_stage(stage_recv, third, 2)
        forward(thirds[third], 8, 2 * third + 1, 16, 48).start()

    for copy in itertools.chain(*schur_copies[:1]):
        copy.start()

    def await_forward(third):
        forward(thirds[third], 8, 2 * third, 0, 16).wait()
        forward(thirds[third], 8, 2 * third + 1, 16, 48).wait()

    await_forward(0)
    await_forward(1)
    packed = [buf[:, r, :] for buf in (coarse_a, coarse_b) for r in range(8)]
    high, low = split(jnp.concatenate(packed, axis=0))
    found = dot(pick, jnp.concatenate([high, low], axis=1))
    found = found[:, 0:LANES] + found[:, LANES : 2 * LANES]
    at = iota((144, LANES), 1) - 1
    from_a = take_lanes(found[0:144], jnp.clip(at + jnp.where(third_of == 1, 64, 0), 0, LANES - 1))
    from_t = take_lanes(found[144:288], jnp.clip(at + 8 * third_of, 0, LANES - 1))
    window = jnp.where(at < 64, from_a, from_t)
    table[...] = jnp.where((at >= 0) & (at < WIN), window, 0.0)
    bases[...] = jnp.broadcast_to((owner - 1) * OWN - 1, (144, LANES))

    def build(first, count):
        @pl.loop(0, 8, unroll=2)
        def _(e):
            everyone = [id_rows[pl.ds(8 * r + e, 1), :] for r in range(6)]
            for k in range(first, first + count, 16):
                rows = table[k : k + 16]
                base = bases[k : k + 16]
                out = pl.ds(pl.multiple_of(k // 48 * 384 + e * 48 + k % 48, 16), 16)
                for r in range(6):
                    place = jnp.broadcast_to(everyone[r], (16, LANES)) - base
                    top, rest = split(take_lanes(rows, jnp.clip(place, 0, LANES - 1)))
                    operator[out, r * LANES : (r + 1) * LANES] = top
                    operator[out, (r + 6) * LANES : (r + 7) * LANES] = rest

    await_forward(2)
    id_rows[...] = jnp.transpose(buf1[:, 6, :])[0:48].astype(I32)
    build(0, 96)
    for third in range(3):
        for stage in range(3):
            await_stage(stage_send, third, stage)

    def gathered(buf):
        top, rest = split(jnp.concatenate([buf[:, r, :] for r in range(6)], axis=0))
        both = jnp.concatenate([top, rest], axis=1)
        return jnp.concatenate([both, both], axis=0)

    def spread(everyone, first, count):
        padded = []
        lanes = iota((48, 2 * LANES), 1) % LANES // 16
        for pair in range(first, first + count):
            solved = jnp.zeros((48, 2 * LANES), F32)
            for half in range(2):
                at = 384 * pair + 192 * half
                product = dot(operator[at : at + 192], everyone)
                for e in range(4):
                    solved = jnp.where(lanes == 4 * half + e, product[48 * e : 48 * e + 48], solved)
            solved = solved[:, 0:LANES] + solved[:, LANES : 2 * LANES]
            zero = jnp.zeros((8, LANES), F32)
            padded += [solved[0:24], zero, solved[24:48], zero]
        if count == 1:
            padded.append(jnp.zeros((64, LANES), F32))
        turned = jnp.transpose(jnp.concatenate(padded, axis=0))
        by_case = turned[0:CASES]
        for e in range(1, 8):
            by_case = by_case + turned[CASES * e : CASES * e + CASES]
        stack = []
        for j in range(2 * count):
            stack += list(split(jnp.where(lane16 // 32 == j, by_case, 0.0)))
        stack = jnp.concatenate(stack, axis=0)
        maps = slice(64 * first, 64 * first + LANES)
        product = dot(stack, map_high[maps]) + dot(stack, map_low[maps])
        return [
            product[32 * j : 32 * j + 16] + product[32 * j + 16 : 32 * j + 32]
            for j in range(2 * count)
        ]

    def around(everyone):
        own0, own1, before, after = spread(everyone, 0, 2)
        return [before, own0, own1, after]

    def add(first, second):
        return [a + b for a, b in zip(first, second)]

    r0 = jumped(add(around(gathered(buf1)), extended(0)))
    send_halo(1, [times(schur_parts, r0[s], s) for s in range(2)])
    for copy in itertools.chain(*schur_copies[1:]):
        copy.start()
    a = [0.5 * v for v in jumped(extended(1))]

    buf2[0] = corner_rows(a)
    to_all(buf2, 6, 6)
    field[2, 0] = times(inverse_parts, a[0], 0)
    field[2, 1] = times(inverse_parts, a[1], 1)
    for copy in wide_copies:
        copy.start()
    build(96, 48)
    for copy in itertools.chain(*schur_copies):
        copy.wait()

    @pl.loop(0, 2)
    def _(i):
        for b in range(4):
            for c in range(4):
                first, last = min(b, c) * LANES, max(b, c) * LANES
                block = schur_side[i, first : first + LANES, last : last + LANES]
                top, rest = split(block if b <= c else jnp.transpose(block))
                columns = slice(c * LANES, (c + 1) * LANES)
                side_parts[i, b * LANES : (b + 1) * LANES, columns] = top
                side_parts[i, DOFS + b * LANES : DOFS + (b + 1) * LANES, columns] = rest

    for copy in wide_copies:
        copy.wait()
    from_all(buf2, 6, 6)

    everyone = gathered(buf2)
    near = around(everyone)
    near = add(near, [halo_wide[0, 1], field[2, 0], field[2, 1], halo_wide[1, 0]])
    far = add(spread(everyone, 2, 1), [halo_wide[0, 0], halo_wide[1, 1]])
    s_a = [far[0], *near, far[1]]
    side_partners = [
        partner_side[0][1:2] - (2 * me - 2) * DOFS, partner_side[1][0:1] - (2 * me + 1) * DOFS
    ]
    partners4 = [side_partners[0], *own_partners, side_partners[1]]
    q4 = [2.0 * jump(s_a[j : j + 3], partners4[j]) for j in range(4)]
    w = [
        0.5 * v
        for v in jumped(
            [
                times(side_parts, q4[0], 0), times(schur_parts, q4[1], 0),
                times(schur_parts, q4[2], 1), times(side_parts, q4[3], 1),
            ]
        )
    ]
    s_a, q = s_a[2:4], q4[1:3]
    dots = as_row(products(r0, a), 0) + as_row(products(a, q), 1)

    buf3[0] = jnp.where(row8 == 6, dots, corner_rows(w))
    to_all(buf3, 7, 7)
    send_halo(4, [times(inverse_parts, w[s], s) for s in range(2)])
    solved_w = extended(4)
    from_all(buf3, 7, 7)

    everyone = gathered(buf3)
    s_w = add(spread(everyone, 0, 1), solved_w[1:3])
    total = jnp.sum(buf3[:, 6, :], axis=0, keepdims=True)
    current, curvature = as_column(total, 0), as_column(total, 1)
    step0 = current / curvature
    r1 = [r0[s] - step0 * q[s] for s in range(2)]
    z1 = [a[s] - step0 * w[s] for s in range(2)]
    s_z = [s_a[s] - step0 * s_w[s] for s in range(2)]
    cross = 4.0 * (products(z1, s_a) + products(a, s_z))
    dots = as_row(products(r1, z1), 0) + as_row(4.0 * products(z1, s_z), 1) + as_row(cross, 2)
    buf4[0] = jnp.where(row8 == 0, dots, 0.0)
    for o in CHIPS:
        for c in range(2):
            if place_of(o) + c > 0:
                pltpu.make_async_remote_copy(
                    src_ref=buf4.at[0, pl.ds(0, 1)],
                    dst_ref=buf4.at[place_of(o) + 64 * c, pl.ds(0, 1)],
                    send_sem=all_send.at[8], recv_sem=all_recv.at[8],
                    device_id=device(o, c), device_id_type=MESH,
                ).start()
    before, after = add(spread(everyone, 1, 1), [solved_w[0], solved_w[3]])
    u = [2.0 * v for v in jumped([before, *s_w, after])]
    image = [q[s] - step0 * u[s] for s in range(2)]
    await_bytes(buf4.at[pl.ds(0, 127), pl.ds(0, 1)], all_recv.at[8])
    total = jnp.sum(buf4[:, 0, :], axis=0, keepdims=True)
    following = as_column(total, 0)
    ratio = following / current
    curvature1 = as_column(total, 1) + ratio * as_column(total, 2) + ratio * ratio * curvature
    step1 = following / curvature1
    for s in range(2):
        mult_ref[:, s, :] = step0 * a[s] + step1 * (z1[s] + ratio * a[s])
        resid_ref[:, s, :] = r1[s] - step1 * (image[s] + ratio * q[s])

    await_bytes(buf4.at[pl.ds(0, 127), pl.ds(0, 1)], all_send.at[8])


def per_device(load, schur_inverse, schur, corner_map, corner_ids, coarse_inverse, partner):
    vmem = pltpu.VMEM
    dma = pltpu.SemaphoreType.DMA
    out = jax.ShapeDtypeStruct(load.shape, F32)
    inputs = (load, schur_inverse, schur, corner_map, corner_ids, coarse_inverse, partner)
    parts = vmem((2, 2 * DOFS, DOFS), BF16)
    slots = vmem((128, 8, LANES), F32)
    return pl.pallas_call(
        kernel,
        out_shape=(out, out),
        in_specs=[pl.BlockSpec(memory_space=pltpu.HBM)] * 7,
        out_specs=(pl.BlockSpec(memory_space=vmem),) * 2,
        scratch_shapes=[
            *(vmem(v.shape, v.dtype) for v in inputs),
            parts, parts,
            vmem((256, DOFS), BF16), vmem((256, DOFS), BF16),
            vmem((2, 2, CORNERS, DOFS), F32), vmem((2, 1, LANES), F32),
            vmem((2, 2, DOFS), I32), vmem((2, DOFS, DOFS), F32), parts,
            vmem((144, LANES), F32), vmem((144, LANES), I32), vmem((48, LANES), I32),
            vmem((1152, 1536), BF16),
            vmem((5, 2, CASES, DOFS), F32), vmem((5, 2, CASES, DOFS), F32),
            vmem((2, 2, CASES, DOFS), F32),
            slots, slots, slots, slots, slots, slots,
            dma((7,)), dma((3, 3)), dma((3, 3)), dma((9,)), dma((9,)), dma((8,)), dma((8,)),
            dma((5, 2)), dma((5, 2)), dma((8, 2)), dma((8, 2)),
        ],
        compiler_params=pltpu.CompilerParams(
            collective_id=0, has_side_effects=True, vmem_limit_bytes=63 << 20
        ),
    )(*inputs)


def solution(mesh):
    in_specs = (
        P(None, "sub", None),
        P("sub", None, None),
        P("sub", None, None),
        P("sub", None, None),
        P("sub", None),
        P("sub", None),
        P("sub", None),
    )
    out_specs = (P(None, "sub", None), P(None, "sub", None))
    return jax.shard_map(
        per_device, mesh=mesh, in_specs=in_specs, out_specs=out_specs, check_vma=False
    )
```
